256 devices in a mesh: shot: 16 (over y, x), recv: 16 (over z, core).
Axes of the slice: x: 4, y: 4, z: 8, core: 2. Of those that a mesh axis runs over, the one named last changes fastest.
Arguments:
- traces: bfloat16 [256, 2048, 128], P('shot', 'recv'), may hold values from -6 to 6
- source_ids: int32 [256], P('shot'), may hold values from 0 to 255, as said below
- taper_ids: int32 [256], P('shot'), may hold values from 0 to 3
- recv_jitter: float32 [2, 2048], replicated, may hold values from -1 to 1
- aperture: int32 [16, 5], replicated, may hold values from -1 to 63, as said below
Outputs:
- multiples: bfloat16 [2, 64, 256, 2048], P(None, None, 'shot', 'recv')
The draws below stay inside these ranges and needn't reach their ends.
Inputs may be any that keep to these rules, and one draw needn't show every extreme that they name: `source_ids`: A permutation of the source numbers. Of the 16 gathers of one shot index at most 2 have numbers in one block of 16 consecutive numbers, and exactly 2 in some block. `aperture`: row j names strips of distinct tiles, each within 3 tiles of j (strip g lies in tile g // 4); entry 0 is a strip of tile j itself; used entries come first, then -1. Every row uses 2 or more entries, and some row uses all 5.
All inputs are finite; a program needn't handle non-finite values.
Results may differ from the reference program's by a relative error of at most 0.0067.
Values may be sent and summed in bfloat16 or wider, within the bound.
A program may use at most 64 MiB of HBM per device.

```python
import math
import jax
import jax.numpy as jnp
import numpy as np
from jax import lax

FREQS = 64
SAMPLES = 128
SRC_DEV = 16
RECV_DEV = 128
STRIPS = 4
APER = 5
HALF = 3
TAPERS = 4
SOURCES = 256
RECEIVERS = 2048


def tile_permutations(key, groups, length):
    return jax.vmap(lambda sub_key: jax.random.permutation(sub_key, length))(jax.random.split(key, groups))


def draw_source_ids(key, part):
    key = jax.random.fold_in(key, 11)
    shots = SOURCES // SRC_DEV
    capacity = 2 * SRC_DEV // shots
    remaining = SRC_DEV - capacity
    profile = [capacity] + [remaining // (shots - 1) + (1 if column < remaining % (shots - 1) else 0) for column in range(shots - 1)]
    tile_of = np.zeros((shots, SRC_DEV), np.int32)
    rank_of = np.zeros((shots, SRC_DEV), np.int32)
    first_rank = [0] * shots
    for sender in range(shots):
        cursor = 0
        for owner_tile in range(shots):
            amount = profile[(owner_tile - sender) % shots]
            tile_of[sender, cursor:cursor + amount] = owner_tile
            rank_of[sender, cursor:cursor + amount] = np.arange(first_rank[owner_tile], first_rank[owner_tile] + amount)
            first_rank[owner_tile] += amount
            cursor += amount
    key_tiles, key_shuffle = jax.random.split(key)
    tile_perms = tile_permutations(key_tiles, shots, SRC_DEV)
    source_list = jnp.asarray(tile_of) * SRC_DEV + tile_perms[jnp.asarray(tile_of), jnp.asarray(rank_of)]
    shuffles = tile_permutations(key_shuffle, shots, SRC_DEV)
    source_list = jnp.take_along_axis(source_list, shuffles, axis=1)
    return source_list.reshape(-1).astype(jnp.int32)


def draw_aperture(key, part):
    key = jax.random.fold_in(key, 23)
    tile_count = RECEIVERS // RECV_DEV
    key_order, key_count, key_strip = jax.random.split(key, 3)
    offsets = np.array([shift_value for shift_value in range(-HALF, HALF + 1) if shift_value != 0], np.int32)
    columns = 2 * HALF
    tile_index = jnp.arange(tile_count, dtype=jnp.int32)[:, None]
    targets = tile_index + jnp.asarray(offsets)[None, :]
    inside = (targets >= 0) & (targets < tile_count)
    scores = jax.random.randint(key_order, (tile_count, columns), 0, 1 << 16) * 16 + jnp.arange(columns, dtype=jnp.int32)[None, :]
    scores = jnp.where(inside, scores, scores + (1 << 22))
    order = jnp.argsort(scores, axis=1, stable=True)
    sorted_targets = jnp.take_along_axis(targets, order, axis=1)
    available = jnp.sum(inside.astype(jnp.int32), axis=1)
    wanted = jax.random.randint(key_count, (tile_count,), 1, APER)
    wanted = jnp.where(tile_index[:, 0] == tile_count // 2, APER - 1, wanted)
    others = jnp.minimum(wanted, available)
    owners = jnp.concatenate([tile_index, sorted_targets[:, :APER - 1]], axis=1)
    used = jnp.concatenate([jnp.ones((tile_count, 1), bool), jnp.arange(APER - 1, dtype=jnp.int32)[None, :] < others[:, None]], axis=1)
    strip_pick = jax.random.randint(key_strip, (tile_count, APER), 0, STRIPS)
    return jnp.where(used, owners * STRIPS + strip_pick, -1).astype(jnp.int32)


def plant(values, own_key, least, top_value):
    longest = values.shape.index(max(values.shape))
    spots = []
    for shift in (0, 1):
        where = [jax.random.randint(jax.random.fold_in(own_key, axis), (), 0, length) for axis, length in enumerate(values.shape)]
        where[longest] = (where[longest] + shift) % values.shape[longest]
        spots.append(tuple(where))
    return values.at[spots[0]].set(least).at[spots[1]].set(top_value)


def level_of(rng, shape, cuts, smallest, top_value):
    def one(axis_at, blocks):
        heights = jax.random.uniform(jax.random.fold_in(jax.random.fold_in(rng, 6), axis_at), (blocks,), jnp.float32, smallest / len(cuts), top_value / len(cuts))
        return jnp.repeat(jnp.exp(heights), shape[axis_at] // blocks).reshape((-1,) + (1,) * (len(shape) - axis_at - 1))

    level = one(*cuts[0])
    for cut in cuts[1:]:
        level = level * one(*cut)
    return level


def noise(own_key, extent, scale, bound, cuts=(), held_as=jnp.bfloat16):
    drawn = scale * jax.random.normal(own_key, extent, jnp.float32)
    if cuts:
        drawn = drawn * level_of(own_key, extent, cuts, -0.22, 0.18)
    return jnp.clip(drawn, -bound, bound).astype(held_as)


def setup_inputs(seed: int = 0) -> dict:
    keys = jax.random.split(jax.random.key(seed), 6)
    return {
        "traces": noise(keys[0], (SOURCES, RECEIVERS, SAMPLES), 1.0, 6.0, ((0, 16), (1, 16))),
        "source_ids": draw_source_ids(jax.random.fold_in(keys[5], 71), 0),
        "taper_ids": plant(jax.random.randint(keys[2], (SOURCES,), 0, TAPERS), jax.random.fold_in(keys[2], 1), 0, TAPERS - 1).astype(jnp.int32),
        "recv_jitter": jnp.clip(jax.random.uniform(keys[3], (2, RECEIVERS), jnp.float32, -1.0, 1.0), -1.0, 1.0),
        "aperture": draw_aperture(jax.random.fold_in(keys[5], 71), 0),
    }


onset_parts = 8.0
lateral_jitter = 0.4
crossline_spread = 3.0
depth_units = 8.0
wave_units = 32.0

def taper_windows(length):
    samples = jnp.arange(length, dtype=jnp.float32)
    onsets = jnp.arange(TAPERS, dtype=jnp.float32)[:, None] * (length / onset_parts)
    ramp_value = jnp.clip((samples[None, :] - onsets) / (length / onset_parts), 0.0, 1.0)
    return 0.5 - 0.5 * jnp.cos(jnp.pi * ramp_value)

def dft_table(length, freq_count):
    samples = jnp.arange(length, dtype=jnp.int32)[:, None]
    freq_bins = jnp.arange(freq_count, dtype=jnp.int32)[None, :]
    phase_index = (2 * freq_bins + 1) * samples % (2 * length)
    phase_angle = jnp.pi * phase_index.astype(jnp.float32) / length
    norm_scale = 1.0 / math.sqrt(length)
    dft_values = jnp.concatenate([jnp.cos(phase_angle), -jnp.sin(phase_angle)], axis=1) * norm_scale
    return dft_values.astype(jnp.bfloat16)

def windowed_transform(trace_rows, taper_list):
    length = trace_rows.shape[2]
    windows = taper_windows(length)
    chosen = jnp.zeros((trace_rows.shape[0], length), jnp.float32)
    for taper_index in range(TAPERS):
        chosen = chosen + (taper_list == taper_index).astype(jnp.float32)[:, None] * windows[taper_index][None, :]
    windowed = (trace_rows.astype(jnp.float32) * chosen[:, None, :]).astype(jnp.bfloat16)
    flat_rows = windowed.reshape(-1, length)
    spectra = jnp.dot(flat_rows, dft_table(length, FREQS), preferred_element_type=jnp.float32)
    return spectra.astype(jnp.bfloat16).reshape(trace_rows.shape[0], trace_rows.shape[1], 2 * FREQS)

def green_block(jitter, strip_id, reader_tile, strip_width, tile_width, live_weight):
    strip_start = (strip_id * strip_width).astype(jnp.int32)
    tile_start = (reader_tile * tile_width).astype(jnp.int32)
    strip_jitter = lax.dynamic_slice_in_dim(jitter, strip_start, strip_width, 1)
    local_jitter = lax.dynamic_slice_in_dim(jitter, tile_start, tile_width, 1)
    strip_x = (strip_start + jnp.arange(strip_width, dtype=jnp.int32)).astype(jnp.float32) + lateral_jitter * strip_jitter[0]
    strip_y = crossline_spread * strip_jitter[1]
    local_x = (tile_start + jnp.arange(tile_width, dtype=jnp.int32)).astype(jnp.float32) + lateral_jitter * local_jitter[0]
    local_y = crossline_spread * local_jitter[1]
    delta_x = strip_x[:, None] - local_x[None, :]
    delta_y = strip_y[:, None] - local_y[None, :]
    offset = jnp.sqrt(delta_x * delta_x + delta_y * delta_y)
    distance = jnp.sqrt(offset * offset + depth_units * depth_units)
    reach_units = float((HALF + 1) * tile_width)
    amplitude = jnp.cos(0.5 * jnp.pi * jnp.minimum(offset / reach_units, 1.0)) * live_weight / math.sqrt(APER * strip_width)
    freq_bins = jnp.arange(FREQS, dtype=jnp.float32)[:, None, None] + 0.5
    phase = 2.0 * jnp.pi / wave_units * freq_bins * distance[None, :, :]
    real_part = amplitude[None, :, :] * jnp.cos(phase)
    imag_part = -amplitude[None, :, :] * jnp.sin(phase)
    from_real = jnp.stack([real_part, imag_part], axis=2)
    from_imag = jnp.stack([-imag_part, real_part], axis=2)
    green_values = jnp.stack([from_real, from_imag], axis=2)
    return green_values.reshape(FREQS, 2 * strip_width, 2 * tile_width).astype(jnp.bfloat16)

def reference(traces, source_ids, taper_ids, recv_jitter, aperture):
    total_sources, receivers, length = traces.shape
    tile_count = receivers // RECV_DEV
    strip_width = RECV_DEV // STRIPS
    arranged = jnp.zeros_like(traces).at[source_ids].set(traces)
    arranged_tapers = jnp.zeros_like(taper_ids).at[source_ids].set(taper_ids)
    blocks = arranged.reshape(-1, SRC_DEV, receivers, length)
    taper_blocks = arranged_tapers.reshape(-1, SRC_DEV)

    def transform(block_pair):
        spectra = windowed_transform(block_pair[0], block_pair[1])
        spectra = spectra.reshape(SRC_DEV, receivers, 2, FREQS).transpose(3, 0, 1, 2)
        return spectra.reshape(FREQS, SRC_DEV, 2 * receivers)
    spectra = lax.map(transform, (blocks, taper_blocks))
    spectra = spectra.transpose(1, 0, 2, 3).reshape(FREQS, total_sources, 2 * receivers)

    def one_tile(tile_index):
        entries = aperture[tile_index]
        accumulated = jnp.zeros((FREQS, total_sources, 2 * RECV_DEV), jnp.float32)
        for slot_index in range(APER):
            strip_id = entries[slot_index]
            live_weight = (strip_id >= 0).astype(jnp.float32)
            clipped_strip = jnp.maximum(strip_id, 0).astype(jnp.int32)
            strip_data = lax.dynamic_slice_in_dim(spectra, (clipped_strip * 2 * strip_width).astype(jnp.int32), 2 * strip_width, 2)
            green_table = green_block(recv_jitter, clipped_strip, tile_index, strip_width, RECV_DEV, live_weight)
            accumulated = accumulated + jnp.einsum('fsx,fxy->fsy', strip_data.astype(jnp.float32), green_table.astype(jnp.float32), precision=lax.Precision.HIGHEST)
        return accumulated.astype(jnp.bfloat16)
    result = lax.map(one_tile, jnp.arange(tile_count, dtype=jnp.int32))
    result = result.reshape(tile_count, FREQS, total_sources, 2, RECV_DEV).transpose(3, 1, 2, 0, 4)
    return result.reshape(2, FREQS, total_sources, receivers)
```

```python
import functools
import math

import jax
import jax.numpy as jnp
import numpy as np
from jax import lax
from jax.experimental import pallas as pl
from jax.experimental.pallas import tpu as pltpu
from jax.sharding import PartitionSpec as P

FREQS = 64
STRIPS = 4
APER = 5
HALF = 3
SRC = 16
TILE = 128
STRIP = 32
SLOTS = 2
QUADS = FREQS // 4
PER = 2
CHUNKS = QUADS // PER
DIRS = (-3, -2, -1, 1, 2, 3)
MESH = pl.DeviceIdType.MESH
F32, BF16, I32 = jnp.float32, jnp.bfloat16, jnp.int32


def sine(x):
    z = x * x
    total = jnp.full_like(x, 1.0 / 6227020800.0)
    for term in (-1.0 / 39916800.0, 1.0 / 362880.0, -1.0 / 5040.0, 1.0 / 120.0, -1.0 / 6.0, 1.0):
        total = total * z + term
    return total * x


def cosine(x):
    z = x * x
    total = jnp.full_like(x, 1.0 / 479001600.0)
    for term in (-1.0 / 3628800.0, 1.0 / 40320.0, -1.0 / 720.0, 1.0 / 24.0, -0.5, 1.0):
        total = total * z + term
    return total


def iota(shape, dim):
    return lax.broadcasted_iota(I32, shape, dim)


def choose(which, options, values):
    chosen = values[0]
    for option, value in zip(options[1:], values[1:]):
        chosen = jnp.where(which == option, value, chosen)
    return chosen


def plus(one, two):
    return one[0] * two[0] - one[1] * two[1], one[1] * two[0] + one[0] * two[1]


def kernel(
    shots, tiles, ids, tapers, aperture, jitter, traces, table, out,
    spec, strips, zsend, zrecv, base, state, turn, green, pick, place, lsend, lrecv, asend, arecv,
    zsend_sem, zrecv_sem, lsend_sem, lrecv_sem, asend_sem, arecv_sem,
):
    me = lax.axis_index("shot")
    tile = lax.axis_index("recv")
    barrier = pltpu.get_barrier_semaphore()

    def shot_peer(step):
        return lax.rem(me + step, shots)

    def recv_peer(step):
        return lax.rem(tile + step + tiles, tiles)

    for step in range(1, shots):
        pl.semaphore_signal(barrier, inc=1, device_id={"shot": shot_peer(step)}, device_id_type=MESH)
    for step in DIRS:
        pl.semaphore_signal(barrier, inc=1, device_id={"recv": recv_peer(step)}, device_id_type=MESH)

    taper = jnp.zeros((SRC, TILE), I32)
    for a in range(SRC):
        taper = jnp.where(iota((SRC, TILE), 0) == a, tapers[a], taper)
    ramp = (iota((SRC, TILE), 1) - taper * 16).astype(F32) * (1.0 / 16.0)
    ramp = sine(jnp.clip(ramp, 0.0, 1.0) * (0.5 * math.pi))
    chosen = ramp * ramp

    for a in range(SRC):
        windowed = (traces[a].astype(F32) * chosen[a : a + 1, :]).astype(BF16)
        spec[pl.ds(a, 2 * FREQS, stride=SRC), :] = lax.dot_general(
            table[...], windowed, (((1,), (1,)), ((), ())), preferred_element_type=F32
        )

    wants = []
    for step in DIRS:
        reader = recv_peer(step)
        want = jnp.int32(0)
        for g in range(APER):
            entry = aperture[reader, g]
            want = jnp.where((entry >= 0) & ((entry >> 2) == tile), entry & 3, want)
        wants.append(want)

    row, lane = iota((SRC, TILE), 0), iota((SRC, TILE), 1)
    label = jnp.full((SRC, TILE), -1, I32)
    count = jnp.zeros((SRC, TILE), I32)
    for a in range(SRC):
        hit = row == (ids[a] >> 4)
        label = jnp.where(hit & (count == (lane & 1)), ids[a] & 15, label)
        count = count + hit.astype(I32)
    for t in range(SRC):
        lsend[t] = label[t : t + 1, :]

    pl.semaphore_wait(barrier, shots - 1 + len(DIRS))

    for step in range(1, shots):
        peer = shot_peer(step)
        pltpu.make_async_remote_copy(
            lsend.at[peer], lrecv.at[me], lsend_sem, lrecv_sem, device_id={"shot": peer}, device_id_type=MESH
        ).start()
    lrecv[me] = lsend[me]

    def send_strips(m, carry):
        for q in range(PER):
            quad = m * PER + q
            panel = spec[pl.ds(pl.multiple_of(quad * TILE, TILE), TILE), :].T.astype(BF16)
            strips[quad] = panel.reshape(STRIPS, STRIP, TILE)
            pieces = [strips[quad, s] for s in range(STRIPS)]
            for k in range(len(DIRS)):
                zsend[m, k, q] = choose(wants[k], range(STRIPS), pieces)
        for k, step in enumerate(DIRS):
            pltpu.make_async_remote_copy(
                zsend.at[m, k],
                zrecv.at[m, len(DIRS) - 1 - k],
                zsend_sem,
                zrecv_sem.at[m],
                device_id={"recv": recv_peer(step)},
                device_id_type=MESH,
            ).start()
        return carry

    lax.fori_loop(0, CHUNKS, send_strips, 0)

    lane = iota((8, TILE), 1)
    owner = jnp.zeros((8, TILE), I32)
    for a in range(SRC):
        owner = jnp.where((lane & 15) == a, ids[a] >> 4, owner)
    rank = jnp.zeros((8, TILE), I32)
    for a in range(SRC):
        rank = rank + ((owner == (ids[a] >> 4)) & ((lane & 15) > a)).astype(I32)
    shape = (SRC * 16, TILE)
    row, lane = iota(shape, 0), iota(shape, 1)
    same = (owner[:1] == (row >> 4)) & (rank[:1] == (row & 1)) & (((row >> 1) & 7) == (lane >> 4))
    pick[...] = same.astype(F32).astype(BF16)

    row, lane = iota((STRIP, TILE), 0), iota((STRIP, TILE), 1)
    here = pl.ds(pl.multiple_of(tile * TILE, TILE), TILE)
    local_x = (tile * TILE + lane).astype(F32) + 0.4 * jitter[0:1, here]
    local_y = 3.0 * jitter[1:2, here]
    near = range(-HALF, HALF + 1)
    jitters = [jitter[:, pl.ds(pl.multiple_of(recv_peer(step) * TILE, TILE), TILE)] for step in near]
    sources = []
    for g in range(APER):
        entry = aperture[tile, g]
        live = (entry >= 0).astype(F32)
        sources.append(jnp.where(entry >= 0, (entry >> 2) - tile, 0))
        strip = jnp.maximum(entry, 0)
        there = choose(sources[g], near, jitters)
        mask = lane == row + (strip & 3) * STRIP
        strip_x = jnp.sum(jnp.where(mask, there[0:1], 0.0), axis=1, keepdims=True)
        strip_y = jnp.sum(jnp.where(mask, there[1:2], 0.0), axis=1, keepdims=True)
        dx = (strip * STRIP + row).astype(F32) + 0.4 * strip_x - local_x
        dy = 3.0 * strip_y - local_y
        square = dx * dx + dy * dy
        cut = jnp.minimum(jnp.sqrt(square) * (1.0 / ((HALF + 1) * TILE)), 1.0)
        amp = cosine(cut * (0.5 * math.pi)) * (live / math.sqrt(APER * STRIP))
        turns = jnp.sqrt(square + 64.0) * (0.5 / 32.0)
        quarter = (turns - jnp.floor(turns + 0.5)) * math.pi
        sin_q, cos_q = sine(quarter), cosine(quarter)
        half = (1.0 - 2.0 * sin_q * sin_q, 2.0 * sin_q * cos_q)
        whole = plus(half, half)
        now = half
        for j in range(4):
            base[g, j, 0] = amp * now[0]
            base[g, j, 1] = amp * now[1]
            if j < 3:
                now = plus(now, whole)
        two = plus(whole, whole)
        four = plus(two, two)
        eight = plus(four, four)
        state[g, 0], state[g, 1] = four
        turn[g, 0], turn[g, 1] = eight

    own_strip = aperture[tile, 0] & 3

    def product(m, carry):
        for g in range(APER):
            rows = pl.ds(g * STRIP, STRIP)
            cos_a, sin_a = state[g, 0], state[g, 1]
            for j in range(4):
                cos_b, sin_b = base[g, j, 0], base[g, j, 1]
                cc, ss, sc, cs = cos_a * cos_b, sin_a * sin_b, sin_a * cos_b, cos_a * sin_b
                green[4 + j, rows, 0:TILE] = (cc - ss).astype(BF16)
                green[4 + j, rows, TILE : 2 * TILE] = (-sc - cs).astype(BF16)
                green[3 - j, rows, 0:TILE] = (cc + ss).astype(BF16)
                green[3 - j, rows, TILE : 2 * TILE] = (cs - sc).astype(BF16)
            state[g, 0], state[g, 1] = plus((cos_a, sin_a), (turn[g, 0], turn[g, 1]))

        pltpu.make_async_copy(zrecv.at[m], zrecv.at[m], zrecv_sem.at[m]).wait()
        panels = []
        for q in range(PER):
            arrived = [zrecv[m, k, q] for k in range(len(DIRS))]
            pieces = [choose(own_strip, range(STRIPS), [strips[m * PER + q, s] for s in range(STRIPS)])]
            for g in range(1, APER):
                pieces.append(choose(sources[g], DIRS, arrived))
            panel = jnp.concatenate(pieces, axis=0).T
            parts = []
            for f in range(4):
                both = jnp.dot(
                    panel[2 * SRC * f : 2 * SRC * (f + 1)], green[4 * q + f], preferred_element_type=F32
                )
                parts.append(both[:SRC, :TILE] - both[SRC:, TILE:])
                parts.append(both[:SRC, TILE:] + both[SRC:, :TILE])
            panels.append(jnp.concatenate(parts, axis=0).astype(BF16))
        slots = jnp.dot(pick[...], jnp.concatenate(panels, axis=1), preferred_element_type=F32).astype(BF16)
        for q in range(PER):
            asend[m, :, 16 * q : 16 * (q + 1), :] = slots[:, TILE * q : TILE * (q + 1)].reshape(SRC, 16, TILE)
        for step in range(1, shots):
            peer = shot_peer(step)
            pltpu.make_async_remote_copy(
                asend.at[m, peer],
                arecv.at[m, me],
                asend_sem,
                arecv_sem.at[m],
                device_id={"shot": peer},
                device_id_type=MESH,
            ).start()
        arecv[m, me] = asend[m, me]
        return carry

    lax.fori_loop(0, CHUNKS, product, 0)

    pltpu.make_async_copy(lrecv.at[pl.ds(0, shots - 1)], lrecv.at[pl.ds(0, shots - 1)], lrecv_sem).wait()
    row, lane = iota((TILE, TILE), 0), iota((TILE, TILE), 1)
    for h in range(2):
        label = jnp.zeros((1, TILE), I32)
        for j in range(8):
            label = jnp.where(iota((1, TILE), 1) >> 4 == j, lrecv[8 * h + j], label)
        same = (label == (row & 15)) & (((lane >> 2) & 3) == ((row >> 4) & 3)) & (((lane >> 1) & 1) == (row >> 6))
        place[:, TILE * h : TILE * (h + 1)] = same.astype(F32).astype(BF16)

    def finish(m, carry):
        part = arecv.at[m, pl.ds(0, shots - 1)]
        pltpu.make_async_copy(part, part, arecv_sem.at[m]).wait()
        blocks = [arecv[m, :, 16 * q : 16 * (q + 1), :].reshape(SRC * 16, TILE) for q in range(PER)]
        done = jnp.dot(place[...], jnp.concatenate(blocks, axis=1), preferred_element_type=F32).astype(BF16)
        for q in range(PER):
            for c in range(2):
                out[c, pl.ds((m * PER + q) * 4, 4)] = done[
                    64 * c : 64 * (c + 1), TILE * q : TILE * (q + 1)
                ].reshape(4, SRC, TILE)
        return carry

    lax.fori_loop(0, CHUNKS, finish, 0)

    pltpu.make_async_copy(zsend, zsend, zsend_sem).wait()
    part = lsend.at[pl.ds(0, shots - 1)]
    pltpu.make_async_copy(part, part, lsend_sem).wait()
    part = asend.at[:, pl.ds(0, shots - 1)]
    pltpu.make_async_copy(part, part, asend_sem).wait()


def dft_table():
    samples = np.arange(TILE)[None, :]
    bins = np.arange(FREQS)[:, None]
    angle = np.pi * ((2 * bins + 1) * samples % (2 * TILE)) / TILE
    values = np.stack([np.cos(angle), -np.sin(angle)], axis=1) / math.sqrt(TILE)
    return values.reshape(2 * FREQS, TILE)


def local(shots, tiles, traces, source_ids, taper_ids, recv_jitter, aperture):
    smem = pl.BlockSpec(memory_space=pltpu.SMEM)
    vmem = pl.BlockSpec(memory_space=pltpu.VMEM)
    table = jnp.asarray(dft_table(), BF16)
    dirs = len(DIRS)
    return pl.pallas_call(
        functools.partial(kernel, shots, tiles),
        out_shape=jax.ShapeDtypeStruct((2, FREQS, SRC, TILE), BF16),
        in_specs=[smem, smem, smem, vmem, vmem, vmem],
        out_specs=vmem,
        scratch_shapes=[
            pltpu.VMEM((2 * FREQS * SRC, TILE), F32),
            pltpu.VMEM((QUADS, STRIPS, STRIP, TILE), BF16),
            pltpu.VMEM((CHUNKS, dirs, PER, STRIP, TILE), BF16),
            pltpu.VMEM((CHUNKS, dirs, PER, STRIP, TILE), BF16),
            pltpu.VMEM((APER, 4, 2, STRIP, TILE), F32),
            pltpu.VMEM((APER, 2, STRIP, TILE), F32),
            pltpu.VMEM((APER, 2, STRIP, TILE), F32),
            pltpu.VMEM((4 * PER, APER * STRIP, 2 * TILE), BF16),
            pltpu.VMEM((SRC * 16, TILE), BF16),
            pltpu.VMEM((TILE, SRC * 16), BF16),
            pltpu.VMEM((SRC, 1, TILE), I32),
            pltpu.VMEM((SRC, 1, TILE), I32),
            pltpu.VMEM((CHUNKS, SRC, 16 * PER, TILE), BF16),
            pltpu.VMEM((CHUNKS, SRC, 16 * PER, TILE), BF16),
            pltpu.SemaphoreType.DMA,
            pltpu.SemaphoreType.DMA((CHUNKS,)),
            pltpu.SemaphoreType.DMA,
            pltpu.SemaphoreType.DMA,
            pltpu.SemaphoreType.DMA,
            pltpu.SemaphoreType.DMA((CHUNKS,)),
        ],
        compiler_params=pltpu.CompilerParams(
            collective_id=0, has_side_effects=True, vmem_limit_bytes=40 * 1024 * 1024
        ),
    )(source_ids, taper_ids, aperture, recv_jitter, traces, table)


def solution(mesh):
    placed = (P("shot", "recv", None), P("shot"), P("shot"), P(), P())
    return jax.shard_map(
        functools.partial(local, mesh.shape["shot"], mesh.shape["recv"]),
        mesh=mesh,
        in_specs=placed,
        out_specs=P(None, None, "shot", "recv"),
        check_vma=False,
    )
```

```python
import functools
import math

import jax
import jax.numpy as jnp
import numpy as np
from jax import lax
from jax.experimental import pallas as pl
from jax.experimental.pallas import tpu as pltpu
from jax.sharding import PartitionSpec as P

FREQS = 64
STRIPS = 4
APER = 5
HALF = 3
SRC = 16
TILE = 128
STRIP = 32
SLOTS = 2
QUADS = FREQS // 4
PER = 2
CHUNKS = QUADS // PER
LATE = 2
EARLY = CHUNKS - LATE
LEAD = 6
LOADS = 4
HOLD = 2
OFFSETS = sorted(
    ((dy, dx) for dy in range(4) for dx in range(4) if dy or dx),
    key=lambda o: -(min(o[0], 4 - o[0]) + min(o[1], 4 - o[1])),
)
DIRS = (-3, -2, -1, 1, 2, 3)
MESH = pl.DeviceIdType.MESH
F32, BF16, I32 = jnp.float32, jnp.bfloat16, jnp.int32


def sine(x):
    z = x * x
    total = jnp.full_like(x, 1.0 / 6227020800.0)
    for term in (-1.0 / 39916800.0, 1.0 / 362880.0, -1.0 / 5040.0, 1.0 / 120.0, -1.0 / 6.0, 1.0):
        total = total * z + term
    return total * x


def cosine(x):
    z = x * x
    total = jnp.full_like(x, 1.0 / 479001600.0)
    for term in (-1.0 / 3628800.0, 1.0 / 40320.0, -1.0 / 720.0, 1.0 / 24.0, -0.5, 1.0):
        total = total * z + term
    return total


def iota(shape, dim):
    return lax.broadcasted_iota(I32, shape, dim)


def choose(which, options, values):
    chosen = values[0]
    for option, value in zip(options[1:], values[1:]):
        chosen = jnp.where(which == option, value, chosen)
    return chosen


def plus(one, two):
    return one[0] * two[0] - one[1] * two[1], one[1] * two[0] + one[0] * two[1]


def kernel(
    tiles, ids_in, tapers_in, aperture_in, jitter_in, traces_in, table_in, out,
    ids, tapers, aperture, jitter, traces, table,
    spec, strips, zsend, zrecv, base, state, turn, green, pick, place, lsend, lrecv, asend, arecv,
    load_sem, zsend_sem, zrecv_sem, label_sem, asend_sem, arecv_sem,
):
    me = lax.axis_index("shot")
    tile = lax.axis_index("recv")
    my_y, my_x = me >> 2, me & 3
    barrier = pltpu.get_barrier_semaphore()

    def shot_peer(offset):
        return ((my_y + offset[0]) & 3) * 4 + ((my_x + offset[1]) & 3)

    def at_shot(peer):
        return {"device_id": {"shot": peer}, "device_id_type": MESH}

    def exists(step):
        return (tile + step >= 0) & (tile + step < tiles)

    loads = [
        pltpu.make_async_copy(ids_in, ids, load_sem.at[0]),
        pltpu.make_async_copy(tapers_in, tapers, load_sem.at[1]),
        pltpu.make_async_copy(aperture_in, aperture, load_sem.at[2]),
        pltpu.make_async_copy(jitter_in, jitter, load_sem.at[3]),
        pltpu.make_async_copy(table_in, table, load_sem.at[4]),
    ]
    part = SRC // LOADS
    for p in range(LOADS):
        rows = pl.ds(p * part, part)
        loads.append(pltpu.make_async_copy(traces_in.at[rows], traces.at[rows], load_sem.at[5 + p]))
    for load in loads:
        load.start()

    for offset in OFFSETS:
        pl.semaphore_signal(barrier, inc=1, **at_shot(shot_peer(offset)))
    peers = jnp.int32(len(OFFSETS))
    for step in DIRS:
        peers = peers + exists(step).astype(I32)

        @pl.when(exists(step))
        def _():
            pl.semaphore_signal(barrier, inc=1, device_id={"recv": tile + step}, device_id_type=MESH)

    for load in loads[:5]:
        load.wait()

    taper = jnp.zeros((SRC, TILE), I32)
    for a in range(SRC):
        taper = jnp.where(iota((SRC, TILE), 0) == a, tapers[a], taper)
    ramp = (iota((SRC, TILE), 1) - taper * 16).astype(F32) * (1.0 / 16.0)
    ramp = sine(jnp.clip(ramp, 0.0, 1.0) * (0.5 * math.pi))
    chosen = ramp * ramp

    lane = iota((8, TILE), 1)
    owner = jnp.zeros((8, TILE), I32)
    for a in range(SRC):
        owner = jnp.where((lane & 15) == a, ids[a] >> 4, owner)
    rank = jnp.zeros((8, TILE), I32)
    for a in range(SRC):
        rank = rank + ((owner == (ids[a] >> 4)) & ((lane & 15) > a)).astype(I32)
    shape = (SRC * 16, TILE)
    row, lane = iota(shape, 0), iota(shape, 1)
    same = (owner[:1] == (row >> 4)) & (rank[:1] == (row & 1)) & (((row >> 1) & 7) == (lane >> 4))
    pick[...] = same.astype(F32).astype(BF16)

    for a in range(SRC):
        if a % part == 0:
            loads[5 + a // part].wait()
        windowed = (traces[a].astype(F32) * chosen[a : a + 1, :]).astype(BF16)
        spec[pl.ds(a, 2 * FREQS, stride=SRC), :] = lax.dot_general(
            table[...], windowed, (((1,), (1,)), ((), ())), preferred_element_type=F32
        )

    wants = []
    for step in DIRS:
        reader = lax.rem(tile + step + tiles, tiles)
        want = jnp.int32(0)
        for g in range(APER):
            entry = aperture[g, reader]
            want = jnp.where((entry >= 0) & ((entry >> 2) == tile), entry & 3, want)
        wants.append(want)

    def split_strips(m, q, panel):
        quad = m * PER + q
        strips[quad] = panel.T.astype(BF16).reshape(STRIPS, STRIP, TILE)
        pieces = [strips[quad, s] for s in range(STRIPS)]
        for k in range(len(DIRS)):
            zsend[m, k, q] = choose(wants[k], range(STRIPS), pieces)

    def spec_panel(m, q):
        return spec[pl.ds(pl.multiple_of((m * PER + q) * TILE, TILE), TILE), :]

    def send_strips(m):
        for k, step in enumerate(DIRS):

            @pl.when(exists(step))
            def _():
                pltpu.make_async_remote_copy(
                    zsend.at[m, k],
                    zrecv.at[m, len(DIRS) - 1 - k],
                    zsend_sem.at[k],
                    zrecv_sem.at[m, len(DIRS) - 1 - k],
                    device_id={"recv": tile + step},
                    device_id_type=MESH,
                ).start()

    def early_strips(m):
        for q in range(PER):
            split_strips(m, q, spec_panel(m, q))
        send_strips(m)

    def send_rows(m, panels):
        slots = jnp.dot(pick[...], jnp.concatenate(panels, axis=1), preferred_element_type=F32).astype(BF16)
        for q in range(PER):
            asend[m, :, 16 * q : 16 * (q + 1), :] = slots[:, TILE * q : TILE * (q + 1)].reshape(SRC, 16, TILE)
        for offset in OFFSETS:
            peer = shot_peer(offset)
            pltpu.make_async_remote_copy(
                asend.at[m, peer], arecv.at[m, me], asend_sem, arecv_sem.at[m], **at_shot(peer)
            ).start()
        arecv[m, me] = asend[m, me]

    def placed_rows(m):
        most = arecv.at[m, pl.ds(0, SRC - 1)]
        pltpu.make_async_copy(most, most, arecv_sem.at[m]).wait()
        blocks = [arecv[m, :, 16 * q : 16 * (q + 1), :].reshape(SRC * 16, TILE) for q in range(PER)]
        rows = jnp.dot(place[...], jnp.concatenate(blocks, axis=1), preferred_element_type=F32)
        return [rows[:, TILE * q : TILE * (q + 1)] for q in range(PER)]

    for q in range(PER):
        split_strips(0, q, spec_panel(0, q))
    pl.semaphore_wait(barrier, peers)
    send_strips(0)
    for m in range(EARLY, CHUNKS):
        send_rows(m, [spec_panel(m, q).astype(BF16) for q in range(PER)])
    for m in range(1, LEAD):
        early_strips(m)

    row, lane = iota((SRC, TILE), 0), iota((SRC, TILE), 1)
    label = jnp.full((SRC, TILE), -1, I32)
    count = jnp.zeros((SRC, TILE), I32)
    for a in range(SRC):
        hit = row == (ids[a] >> 4)
        label = jnp.where(hit & (count == (lane & 1)), ids[a] & 15, label)
        count = count + hit.astype(I32)
    for t in range(SRC):
        lsend[t] = label[t : t + 1, :]
    lrecv[me] = lsend[me]
    for offset in OFFSETS:
        peer = shot_peer(offset)
        pltpu.make_async_remote_copy(
            lsend.at[peer], lrecv.at[me], label_sem.at[0], label_sem.at[1], **at_shot(peer)
        ).start()

    row, lane = iota((STRIP, TILE), 0), iota((STRIP, TILE), 1)
    here = pl.ds(pl.multiple_of(tile * TILE, TILE), TILE)
    local_x = (tile * TILE + lane).astype(F32) + 0.4 * jitter[0:1, here]
    local_y = 3.0 * jitter[1:2, here]
    near = (0,) + DIRS
    jitters = []
    for step in near:
        there = lax.rem(tile + step + tiles, tiles)
        jitters.append(jitter[:, pl.ds(pl.multiple_of(there * TILE, TILE), TILE)])
    sources = []
    for g in range(APER):
        entry = aperture[g, tile]
        live = (entry >= 0).astype(F32)
        sources.append(jnp.where(entry >= 0, (entry >> 2) - tile, 0))
        strip = jnp.maximum(entry, 0)
        there = choose(sources[g], near, jitters)
        mask = lane == row + (strip & 3) * STRIP
        strip_x = jnp.sum(jnp.where(mask, there[0:1], 0.0), axis=1, keepdims=True)
        strip_y = jnp.sum(jnp.where(mask, there[1:2], 0.0), axis=1, keepdims=True)
        dx = (strip * STRIP + row).astype(F32) + 0.4 * strip_x - local_x
        dy = 3.0 * strip_y - local_y
        square = dx * dx + dy * dy
        cut = jnp.minimum(jnp.sqrt(square) * (1.0 / ((HALF + 1) * TILE)), 1.0)
        amp = cosine(cut * (0.5 * math.pi)) * (live / math.sqrt(APER * STRIP))
        turns = jnp.sqrt(square + 64.0) * (0.5 / 32.0)
        quarter = (turns - jnp.floor(turns + 0.5)) * math.pi
        sin_q, cos_q = sine(quarter), cosine(quarter)
        half = (1.0 - 2.0 * sin_q * sin_q, 2.0 * sin_q * cos_q)
        whole = plus(half, half)
        now = half
        for j in range(4):
            base[g, j, 0] = amp * now[0]
            base[g, j, 1] = amp * now[1]
            if j < 3:
                now = plus(now, whole)
        two = plus(whole, whole)
        four = plus(two, two)
        eight = plus(four, four)
        state[g, 0], state[g, 1] = four
        turn[g, 0], turn[g, 1] = eight

    own_strip = aperture[0, tile] & 3

    def make_green():
        for g in range(APER):
            rows = pl.ds(g * STRIP, STRIP)
            cos_a, sin_a = state[g, 0], state[g, 1]
            for j in range(4):
                cos_b, sin_b = base[g, j, 0], base[g, j, 1]
                cc, ss, sc, cs = cos_a * cos_b, sin_a * sin_b, sin_a * cos_b, cos_a * sin_b
                green[4 + j, rows, 0:TILE] = (cc - ss).astype(BF16)
                green[4 + j, rows, TILE : 2 * TILE] = (-sc - cs).astype(BF16)
                green[3 - j, rows, 0:TILE] = (cc + ss).astype(BF16)
                green[3 - j, rows, TILE : 2 * TILE] = (cs - sc).astype(BF16)
            state[g, 0], state[g, 1] = plus((cos_a, sin_a), (turn[g, 0], turn[g, 1]))

    def product(m):
        for k, step in enumerate(DIRS):

            @pl.when(exists(step))
            def _():
                pltpu.make_async_copy(zrecv.at[m, k], zrecv.at[m, k], zrecv_sem.at[m, k]).wait()

        panels = []
        for q in range(PER):
            own = choose(own_strip, range(STRIPS), [strips[m * PER + q, s] for s in range(STRIPS)])
            pieces = [own]
            options = [own] + [zrecv[m, k, q] for k in range(len(DIRS))]
            for g in range(1, APER):
                pieces.append(choose(sources[g], near, options))
            panel = jnp.concatenate(pieces, axis=0).T
            parts = []
            for f in range(4):
                both = jnp.dot(
                    panel[2 * SRC * f : 2 * SRC * (f + 1)], green[4 * q + f], preferred_element_type=F32
                )
                parts.append(both[:SRC, :TILE] - both[SRC:, TILE:])
                parts.append(both[:SRC, TILE:] + both[SRC:, :TILE])
            panels.append(jnp.concatenate(parts, axis=0).astype(BF16))
        return panels

    def store(m, panels):
        for q in range(PER):
            panel = panels[q].astype(BF16).reshape(4, 2, SRC, TILE)
            for c in range(2):
                out[c, pl.ds((m * PER + q) * 4, 4)] = panel[:, c]

    def early(m, carry):
        @pl.when(m + LEAD < EARLY)
        def _():
            early_strips(m + LEAD)

        make_green()
        send_rows(m, product(m))
        return carry

    lax.fori_loop(0, EARLY, early, 0)

    most = lrecv.at[pl.ds(0, SRC - 1)]
    pltpu.make_async_copy(most, most, label_sem.at[1]).wait()
    row, lane = iota((TILE, TILE), 0), iota((TILE, TILE), 1)
    for h in range(2):
        label = jnp.zeros((1, TILE), I32)
        for j in range(8):
            label = jnp.where(iota((1, TILE), 1) >> 4 == j, lrecv[8 * h + j], label)
        same = (label == (row & 15)) & (((lane >> 1) & 7) == (row >> 4))
        place[:, TILE * h : TILE * (h + 1)] = same.astype(F32).astype(BF16)

    def relay(m, carry):
        rows = placed_rows(m)
        for q in range(PER):
            split_strips(m, q, rows[q])
        send_strips(m)
        return carry

    lax.fori_loop(EARLY, CHUNKS, relay, 0)

    def finish(m, carry):
        store(m, placed_rows(m))
        return carry

    lax.fori_loop(0, EARLY - HOLD, finish, 0)

    def late(m, carry):
        make_green()
        store(m, product(m))
        return carry

    lax.fori_loop(EARLY, CHUNKS, late, 0)
    lax.fori_loop(EARLY - HOLD, EARLY, finish, 0)

    for k, step in enumerate(DIRS):

        @pl.when(exists(step))
        def _():
            pltpu.make_async_copy(zsend.at[:, k], zsend.at[:, k], zsend_sem.at[k]).wait()

    most = lsend.at[pl.ds(0, SRC - 1)]
    pltpu.make_async_copy(most, most, label_sem.at[0]).wait()
    most = asend.at[:, pl.ds(0, SRC - 1)]
    pltpu.make_async_copy(most, most, asend_sem).wait()


def dft_table():
    samples = np.arange(TILE)[None, :]
    bins = np.arange(FREQS)[:, None]
    angle = np.pi * ((2 * bins + 1) * samples % (2 * TILE)) / TILE
    values = np.stack([np.cos(angle), -np.sin(angle)], axis=1) / math.sqrt(TILE)
    return values.reshape(2 * FREQS, TILE)


def local(tiles, traces, source_ids, taper_ids, recv_jitter, aperture):
    hbm = pl.BlockSpec(memory_space=pltpu.HBM)
    table = jnp.asarray(dft_table(), BF16)
    dirs = len(DIRS)
    return pl.pallas_call(
        functools.partial(kernel, tiles),
        out_shape=pltpu.VMEM((2, FREQS, SRC, TILE), BF16),
        in_specs=[hbm] * 6,
        out_specs=pl.BlockSpec(memory_space=pltpu.VMEM),
        scratch_shapes=[
            pltpu.SMEM((SRC,), I32),
            pltpu.SMEM((SRC,), I32),
            pltpu.SMEM((APER, tiles), I32),
            pltpu.VMEM(recv_jitter.shape, F32),
            pltpu.VMEM(traces.shape, BF16),
            pltpu.VMEM(table.shape, BF16),
            pltpu.VMEM((2 * FREQS * SRC, TILE), F32),
            pltpu.VMEM((QUADS, STRIPS, STRIP, TILE), BF16),
            pltpu.VMEM((CHUNKS, dirs, PER, STRIP, TILE), BF16),
            pltpu.VMEM((CHUNKS, dirs, PER, STRIP, TILE), BF16),
            pltpu.VMEM((APER, 4, 2, STRIP, TILE), F32),
            pltpu.VMEM((APER, 2, STRIP, TILE), F32),
            pltpu.VMEM((APER, 2, STRIP, TILE), F32),
            pltpu.VMEM((8, APER * STRIP, 2 * TILE), BF16),
            pltpu.VMEM((SRC * 16, TILE), BF16),
            pltpu.VMEM((TILE, SRC * 16), BF16),
            pltpu.VMEM((SRC, 1, TILE), I32),
            pltpu.VMEM((SRC, 1, TILE), I32),
            pltpu.VMEM((CHUNKS, SRC, 16 * PER, TILE), BF16),
            pltpu.VMEM((CHUNKS, SRC, 16 * PER, TILE), BF16),
            pltpu.SemaphoreType.DMA((5 + LOADS,)),
            pltpu.SemaphoreType.DMA((dirs,)),
            pltpu.SemaphoreType.DMA((CHUNKS, dirs)),
            pltpu.SemaphoreType.DMA((2,)),
            pltpu.SemaphoreType.DMA,
            pltpu.SemaphoreType.DMA((CHUNKS,)),
        ],
        compiler_params=pltpu.CompilerParams(
            collective_id=0, has_side_effects=True, vmem_limit_bytes=62 * 1024 * 1024
        ),
    )(source_ids, taper_ids, aperture.T, recv_jitter, traces, table)


def solution(mesh):
    placed = (P("shot", "recv", None), P("shot"), P("shot"), P(), P())
    return jax.shard_map(
        functools.partial(local, mesh.shape["recv"]),
        mesh=mesh,
        in_specs=placed,
        out_specs=P(None, None, "shot", "recv"),
        check_vma=False,
    )
```

```python
import functools
import math

import jax
import jax.numpy as jnp
import numpy as np
from jax import lax
from jax.experimental import pallas as pl
from jax.experimental.pallas import tpu as pltpu
from jax.sharding import PartitionSpec as P

FREQS = 64
STRIPS = 4
APER = 5
HALF = 3
SRC = 16
TILE = 128
STRIP = 32
SLOTS = 2
QUADS = FREQS // 4
PER = 2
CHUNKS = QUADS // PER
LATE = 3
EARLY = CHUNKS - LATE
LOADS = 4
HOLD = 2
SHIFT = 3
OFFSETS = sorted(
    ((dy, dx) for dy in range(4) for dx in range(4) if dy or dx),
    key=lambda o: -(min(o[0], 4 - o[0]) + min(o[1], 4 - o[1])),
)
DIRS = (-3, -2, -1, 1, 2, 3)
DEFER = (3,)
ALL = range(len(DIRS))
NOW = tuple(k for k in ALL if DIRS[k] not in DEFER)
LATER = tuple(k for k in ALL if DIRS[k] in DEFER)
MESH = pl.DeviceIdType.MESH
F32, BF16, I32 = jnp.float32, jnp.bfloat16, jnp.int32


def sine(x):
    z = x * x
    total = jnp.full_like(x, 1.0 / 6227020800.0)
    for term in (-1.0 / 39916800.0, 1.0 / 362880.0, -1.0 / 5040.0, 1.0 / 120.0, -1.0 / 6.0, 1.0):
        total = total * z + term
    return total * x


def cosine(x):
    z = x * x
    total = jnp.full_like(x, 1.0 / 479001600.0)
    for term in (-1.0 / 3628800.0, 1.0 / 40320.0, -1.0 / 720.0, 1.0 / 24.0, -0.5, 1.0):
        total = total * z + term
    return total


def iota(shape, dim):
    return lax.broadcasted_iota(I32, shape, dim)


def choose(which, options, values):
    chosen = values[0]
    for option, value in zip(options[1:], values[1:]):
        chosen = jnp.where(which == option, value, chosen)
    return chosen


def plus(one, two):
    return one[0] * two[0] - one[1] * two[1], one[1] * two[0] + one[0] * two[1]


def kernel(
    tiles, ids_in, tapers_in, aperture_in, jitter_in, traces_in, table_in, out,
    ids, tapers, aperture, jitter, traces, table,
    spec, strips, zsend, zrecv, base, state, turn, green, pick, place, lsend, lrecv, asend, arecv,
    load_sem, zsend_sem, zrecv_sem, label_sem, asend_sem, arecv_sem, ready,
):
    me = lax.axis_index("shot")
    tile = lax.axis_index("recv")
    my_y, my_x = me >> 2, me & 3
    barrier = pltpu.get_barrier_semaphore()

    def shot_peer(offset):
        return ((my_y + offset[0]) & 3) * 4 + ((my_x + offset[1]) & 3)

    def at_shot(peer):
        return {"device_id": {"shot": peer}, "device_id_type": MESH}

    def at_recv(step):
        return {"device_id": {"recv": tile + step}, "device_id_type": MESH}

    def exists(step):
        return (tile + step >= 0) & (tile + step < tiles)

    for offset in OFFSETS:
        pl.semaphore_signal(barrier, inc=1, **at_shot(shot_peer(offset)))
    peers = jnp.int32(len(OFFSETS))
    for step in DIRS:
        if step not in DEFER:
            peers = peers + exists(step).astype(I32)
        if -step in DEFER:
            continue

        @pl.when(exists(step))
        def _():
            pl.semaphore_signal(barrier, inc=1, **at_recv(step))

    loads = [
        pltpu.make_async_copy(ids_in, ids, load_sem.at[0]),
        pltpu.make_async_copy(tapers_in, tapers, load_sem.at[1]),
        pltpu.make_async_copy(aperture_in, aperture, load_sem.at[2]),
        pltpu.make_async_copy(jitter_in, jitter, load_sem.at[3]),
        pltpu.make_async_copy(table_in, table, load_sem.at[4]),
    ]
    part = SRC // LOADS
    for p in range(LOADS):
        rows = pl.ds(p * part, part)
        loads.append(pltpu.make_async_copy(traces_in.at[rows], traces.at[rows], load_sem.at[5 + p]))
    for load in loads:
        load.start()

    for load in loads[:5]:
        load.wait()

    taper = jnp.zeros((SRC, TILE), I32)
    for a in range(SRC):
        taper = jnp.where(iota((SRC, TILE), 0) == a, tapers[a], taper)
    ramp = (iota((SRC, TILE), 1) - taper * 16).astype(F32) * (1.0 / 16.0)
    ramp = sine(jnp.clip(ramp, 0.0, 1.0) * (0.5 * math.pi))
    chosen = ramp * ramp

    lane = iota((8, TILE), 1)
    owner = jnp.zeros((8, TILE), I32)
    for a in range(SRC):
        owner = jnp.where((lane & 15) == a, ids[a] >> 4, owner)
    rank = jnp.zeros((8, TILE), I32)
    for a in range(SRC):
        rank = rank + ((owner == (ids[a] >> 4)) & ((lane & 15) > a)).astype(I32)
    shape = (SRC * 16, TILE)
    row, lane = iota(shape, 0), iota(shape, 1)
    same = (owner[:1] == (row >> 4)) & (rank[:1] == (row & 1)) & (((row >> 1) & 7) == (lane >> 4))
    pick[...] = same.astype(F32).astype(BF16)

    for a in range(SRC):
        if a % part == 0:
            loads[5 + a // part].wait()
        windowed = (traces[a].astype(F32) * chosen[a : a + 1, :]).astype(BF16)
        spec[pl.ds(a, 2 * FREQS, stride=SRC), :] = lax.dot_general(
            table[...], windowed, (((1,), (1,)), ((), ())), preferred_element_type=F32
        )

    wants = []
    for step in DIRS:
        reader = lax.rem(tile + step + tiles, tiles)
        want = jnp.int32(0)
        for g in range(APER):
            entry = aperture[g, reader]
            want = jnp.where((entry >= 0) & ((entry >> 2) == tile), entry & 3, want)
        wants.append(want)

    def split_strips(m, q, panel):
        quad = m * PER + q
        strips[quad] = panel.T.astype(BF16).reshape(STRIPS, STRIP, TILE)
        pieces = [strips[quad, s] for s in range(STRIPS)]
        for k in range(len(DIRS)):
            zsend[m, k, q] = choose(wants[k], range(STRIPS), pieces)

    def spec_panel(m, q):
        return spec[pl.ds(pl.multiple_of((m * PER + q) * TILE, TILE), TILE), :]

    def send_strips(m, which):
        for k in which:
            step = DIRS[k]

            @pl.when(exists(step))
            def _():
                pltpu.make_async_remote_copy(
                    zsend.at[m, k],
                    zrecv.at[m, len(DIRS) - 1 - k],
                    zsend_sem.at[k],
                    zrecv_sem.at[m, len(DIRS) - 1 - k],
                    **at_recv(step),
                ).start()

    def send_rows(m, panels):
        slots = jnp.dot(pick[...], jnp.concatenate(panels, axis=1), preferred_element_type=F32).astype(BF16)
        for q in range(PER):
            asend[m, :, 16 * q : 16 * (q + 1), :] = slots[:, TILE * q : TILE * (q + 1)].reshape(SRC, 16, TILE)
        for offset in OFFSETS:
            peer = shot_peer(offset)
            pltpu.make_async_remote_copy(
                asend.at[m, peer], arecv.at[m, me], asend_sem, arecv_sem.at[m], **at_shot(peer)
            ).start()
        arecv[m, me] = asend[m, me]

    def placed_rows(m):
        most = arecv.at[m, pl.ds(0, SRC - 1)]
        pltpu.make_async_copy(most, most, arecv_sem.at[m]).wait()
        blocks = [arecv[m, :, 16 * q : 16 * (q + 1), :].reshape(SRC * 16, TILE) for q in range(PER)]
        rows = jnp.dot(place[...], jnp.concatenate(blocks, axis=1), preferred_element_type=F32)
        return [rows[:, TILE * q : TILE * (q + 1)] for q in range(PER)]

    for q in range(PER):
        split_strips(0, q, spec_panel(0, q))
    pl.semaphore_wait(barrier, peers)
    for step in DEFER:

        @pl.when(exists(-step))
        def _():
            pl.semaphore_signal(ready.at[step - 1], inc=1, **at_recv(-step))

    send_strips(0, NOW)
    for m in range(EARLY, CHUNKS):
        send_rows(m, [spec_panel(m, q).astype(BF16) for q in range(PER)])
    for m in range(1, EARLY):
        for q in range(PER):
            split_strips(m, q, spec_panel(m, q))
        send_strips(m, NOW)

    row, lane = iota((SRC, TILE), 0), iota((SRC, TILE), 1)
    label = jnp.full((SRC, TILE), -1, I32)
    count = jnp.zeros((SRC, TILE), I32)
    for a in range(SRC):
        hit = row == (ids[a] >> 4)
        label = jnp.where(hit & (count == (lane & 1)), ids[a] & 15, label)
        count = count + hit.astype(I32)
    for t in range(SRC):
        lsend[t] = label[t : t + 1, :]
    lrecv[me] = lsend[me]
    for offset in OFFSETS:
        peer = shot_peer(offset)
        pltpu.make_async_remote_copy(
            lsend.at[peer], lrecv.at[me], label_sem.at[0], label_sem.at[1], **at_shot(peer)
        ).start()

    row, lane = iota((STRIP, TILE), 0), iota((STRIP, TILE), 1)
    here = pl.ds(pl.multiple_of(tile * TILE, TILE), TILE)
    local_x = (tile * TILE + lane).astype(F32) + 0.4 * jitter[0:1, here]
    local_y = 3.0 * jitter[1:2, here]
    near = (0,) + DIRS
    jitters = []
    for step in near:
        there = lax.rem(tile + step + tiles, tiles)
        jitters.append(jitter[:, pl.ds(pl.multiple_of(there * TILE, TILE), TILE)])
    sources = []
    for g in range(APER):
        entry = aperture[g, tile]
        live = (entry >= 0).astype(F32)
        sources.append(jnp.where(entry >= 0, (entry >> 2) - tile, 0))
        strip = jnp.maximum(entry, 0)
        there = choose(sources[g], near, jitters)
        mask = lane == row + (strip & 3) * STRIP
        strip_x = jnp.sum(jnp.where(mask, there[0:1], 0.0), axis=1, keepdims=True)
        strip_y = jnp.sum(jnp.where(mask, there[1:2], 0.0), axis=1, keepdims=True)
        dx = (strip * STRIP + row).astype(F32) + 0.4 * strip_x - local_x
        dy = 3.0 * strip_y - local_y
        square = dx * dx + dy * dy
        cut = jnp.minimum(jnp.sqrt(square) * (1.0 / ((HALF + 1) * TILE)), 1.0)
        amp = cosine(cut * (0.5 * math.pi)) * (live / math.sqrt(APER * STRIP))
        turns = jnp.sqrt(square + 64.0) * (0.5 / 32.0)
        quarter = (turns - jnp.floor(turns + 0.5)) * math.pi
        sin_q, cos_q = sine(quarter), cosine(quarter)
        half = (1.0 - 2.0 * sin_q * sin_q, 2.0 * sin_q * cos_q)
        whole = plus(half, half)
        now = half
        for j in range(4):
            base[g, j, 0] = amp * now[0]
            base[g, j, 1] = amp * now[1]
            if j < 3:
                now = plus(now, whole)
        two = plus(whole, whole)
        four = plus(two, two)
        eight = plus(four, four)
        state[g, 0], state[g, 1] = four
        turn[g, 0], turn[g, 1] = eight

    for step in DEFER:

        @pl.when(exists(step))
        def _():
            pl.semaphore_wait(ready.at[step - 1], 1)

    for m in range(EARLY):
        send_strips(m, LATER)

    own_strip = aperture[0, tile] & 3

    def make_green():
        for g in range(APER):
            rows = pl.ds(g * STRIP, STRIP)
            cos_a, sin_a = state[g, 0], state[g, 1]
            for j in range(4):
                cos_b, sin_b = base[g, j, 0], base[g, j, 1]
                cc, ss, sc, cs = cos_a * cos_b, sin_a * sin_b, sin_a * cos_b, cos_a * sin_b
                green[4 + j, rows, 0:TILE] = (cc - ss).astype(BF16)
                green[4 + j, rows, TILE : 2 * TILE] = (-sc - cs).astype(BF16)
                green[3 - j, rows, 0:TILE] = (cc + ss).astype(BF16)
                green[3 - j, rows, TILE : 2 * TILE] = (cs - sc).astype(BF16)
            state[g, 0], state[g, 1] = plus((cos_a, sin_a), (turn[g, 0], turn[g, 1]))

    def product(m):
        for k, step in enumerate(DIRS):

            @pl.when(exists(step))
            def _():
                pltpu.make_async_copy(zrecv.at[m, k], zrecv.at[m, k], zrecv_sem.at[m, k]).wait()

        panels = []
        for q in range(PER):
            own = choose(own_strip, range(STRIPS), [strips[m * PER + q, s] for s in range(STRIPS)])
            pieces = [own]
            options = [own] + [zrecv[m, k, q] for k in range(len(DIRS))]
            for g in range(1, APER):
                pieces.append(choose(sources[g], near, options))
            panel = jnp.concatenate(pieces, axis=0).T
            parts = []
            for f in range(4):
                both = jnp.dot(
                    panel[2 * SRC * f : 2 * SRC * (f + 1)], green[4 * q + f], preferred_element_type=F32
                )
                parts.append(both[:SRC, :TILE] - both[SRC:, TILE:])
                parts.append(both[:SRC, TILE:] + both[SRC:, :TILE])
            panels.append(jnp.concatenate(parts, axis=0).astype(BF16))
        return panels

    def store(m, panels):
        for q in range(PER):
            panel = panels[q].astype(BF16).reshape(4, 2, SRC, TILE)
            for c in range(2):
                out[c, pl.ds((m * PER + q) * 4, 4)] = panel[:, c]

    def early(m, carry):
        make_green()
        send_rows(m, product(m))
        return carry

    lax.fori_loop(0, SHIFT, early, 0)

    most = lrecv.at[pl.ds(0, SRC - 1)]
    pltpu.make_async_copy(most, most, label_sem.at[1]).wait()
    row, lane = iota((TILE, TILE), 0), iota((TILE, TILE), 1)
    for h in range(2):
        label = jnp.zeros((1, TILE), I32)
        for j in range(8):
            label = jnp.where(iota((1, TILE), 1) >> 4 == j, lrecv[8 * h + j], label)
        same = (label == (row & 15)) & (((lane >> 1) & 7) == (row >> 4))
        place[:, TILE * h : TILE * (h + 1)] = same.astype(F32).astype(BF16)

    def relay(m, carry):
        rows = placed_rows(m)
        for q in range(PER):
            split_strips(m, q, rows[q])
        send_strips(m, ALL)
        return carry

    def both(m, carry):
        relay(EARLY - SHIFT + m, 0)
        early(m, 0)
        return carry

    split = min(EARLY, SHIFT + LATE)
    lax.fori_loop(SHIFT, split, both, 0)
    lax.fori_loop(EARLY - SHIFT + split, CHUNKS, relay, 0)
    lax.fori_loop(split, EARLY, early, 0)

    def finish(m, carry):
        store(m, placed_rows(m))
        return carry

    lax.fori_loop(0, EARLY - HOLD, finish, 0)

    def late(m, carry):
        make_green()
        store(m, product(m))
        return carry

    lax.fori_loop(EARLY, CHUNKS, late, 0)
    lax.fori_loop(EARLY - HOLD, EARLY, finish, 0)

    for k, step in enumerate(DIRS):

        @pl.when(exists(step))
        def _():
            pltpu.make_async_copy(zsend.at[:, k], zsend.at[:, k], zsend_sem.at[k]).wait()

    most = lsend.at[pl.ds(0, SRC - 1)]
    pltpu.make_async_copy(most, most, label_sem.at[0]).wait()
    most = asend.at[:, pl.ds(0, SRC - 1)]
    pltpu.make_async_copy(most, most, asend_sem).wait()


def dft_table():
    samples = np.arange(TILE)[None, :]
    bins = np.arange(FREQS)[:, None]
    angle = np.pi * ((2 * bins + 1) * samples % (2 * TILE)) / TILE
    values = np.stack([np.cos(angle), -np.sin(angle)], axis=1) / math.sqrt(TILE)
    return values.reshape(2 * FREQS, TILE)


def local(tiles, traces, source_ids, taper_ids, recv_jitter, aperture):
    hbm = pl.BlockSpec(memory_space=pltpu.HBM)
    table = jnp.asarray(dft_table(), BF16)
    dirs = len(DIRS)
    return pl.pallas_call(
        functools.partial(kernel, tiles),
        out_shape=pltpu.VMEM((2, FREQS, SRC, TILE), BF16),
        in_specs=[hbm] * 6,
        out_specs=pl.BlockSpec(memory_space=pltpu.VMEM),
        scratch_shapes=[
            pltpu.SMEM((SRC,), I32),
            pltpu.SMEM((SRC,), I32),
            pltpu.SMEM((APER, tiles), I32),
            pltpu.VMEM(recv_jitter.shape, F32),
            pltpu.VMEM(traces.shape, BF16),
            pltpu.VMEM(table.shape, BF16),
            pltpu.VMEM((2 * FREQS * SRC, TILE), F32),
            pltpu.VMEM((QUADS, STRIPS, STRIP, TILE), BF16),
            pltpu.VMEM((CHUNKS, dirs, PER, STRIP, TILE), BF16),
            pltpu.VMEM((CHUNKS, dirs, PER, STRIP, TILE), BF16),
            pltpu.VMEM((APER, 4, 2, STRIP, TILE), F32),
            pltpu.VMEM((APER, 2, STRIP, TILE), F32),
            pltpu.VMEM((APER, 2, STRIP, TILE), F32),
            pltpu.VMEM((8, APER * STRIP, 2 * TILE), BF16),
            pltpu.VMEM((SRC * 16, TILE), BF16),
            pltpu.VMEM((TILE, SRC * 16), BF16),
            pltpu.VMEM((SRC, 1, TILE), I32),
            pltpu.VMEM((SRC, 1, TILE), I32),
            pltpu.VMEM((CHUNKS, SRC, 16 * PER, TILE), BF16),
            pltpu.VMEM((CHUNKS, SRC, 16 * PER, TILE), BF16),
            pltpu.SemaphoreType.DMA((5 + LOADS,)),
            pltpu.SemaphoreType.DMA((dirs,)),
            pltpu.SemaphoreType.DMA((CHUNKS, dirs)),
            pltpu.SemaphoreType.DMA((2,)),
            pltpu.SemaphoreType.DMA,
            pltpu.SemaphoreType.DMA((CHUNKS,)),
            pltpu.SemaphoreType.REGULAR((HALF,)),
        ],
        compiler_params=pltpu.CompilerParams(
            collective_id=0, has_side_effects=True, vmem_limit_bytes=62 * 1024 * 1024
        ),
    )(source_ids, taper_ids, aperture.T, recv_jitter, traces, table)


def solution(mesh):
    placed = (P("shot", "recv", None), P("shot"), P("shot"), P(), P())
    return jax.shard_map(
        functools.partial(local, mesh.shape["recv"]),
        mesh=mesh,
        in_specs=placed,
        out_specs=P(None, None, "shot", "recv"),
        check_vma=False,
    )
```

```python
import functools
import math

import jax
import jax.numpy as jnp
import numpy as np
from jax import lax
from jax.experimental import pallas as pl
from jax.experimental.pallas import tpu as pltpu
from jax.sharding import PartitionSpec as P

FREQS = 64
STRIPS = 4
APER = 5
HALF = 3
SRC = 16
TILE = 128
STRIP = 32
SLOTS = 2
QUADS = FREQS // 4
PER = 2
CHUNKS = QUADS // PER
LATE = 3
EARLY = CHUNKS - LATE
LOADS = 4
HOLD = 3
SHIFT = 3
EAGER = False
OFFSETS = sorted(
    ((dy, dx) for dy in range(4) for dx in range(4) if dy or dx),
    key=lambda o: -(min(o[0], 4 - o[0]) + min(o[1], 4 - o[1])),
)
DIRS = (-3, -2, -1, 1, 2, 3)
GROUPS = ((0, 1), (1, 1), (2, 1), (3, 1), (4, 1))
ALL, NEAR, FAR = range(6), range(5), range(5, 6)
MESH = pl.DeviceIdType.MESH
F32, BF16, I32 = jnp.float32, jnp.bfloat16, jnp.int32


def sine(x):
    z = x * x
    total = jnp.full_like(x, 1.0 / 6227020800.0)
    for term in (-1.0 / 39916800.0, 1.0 / 362880.0, -1.0 / 5040.0, 1.0 / 120.0, -1.0 / 6.0, 1.0):
        total = total * z + term
    return total * x


def cosine(x):
    z = x * x
    total = jnp.full_like(x, 1.0 / 479001600.0)
    for term in (-1.0 / 3628800.0, 1.0 / 40320.0, -1.0 / 720.0, 1.0 / 24.0, -0.5, 1.0):
        total = total * z + term
    return total


def iota(shape, dim):
    return lax.broadcasted_iota(I32, shape, dim)


def choose(which, options, values):
    chosen = values[0]
    for option, value in zip(options[1:], values[1:]):
        chosen = jnp.where(which == option, value, chosen)
    return chosen


def plus(one, two):
    return one[0] * two[0] - one[1] * two[1], one[1] * two[0] + one[0] * two[1]


def kernel(
    tiles, ids_in, tapers_in, aperture_in, jitter_in, traces_in, table_in, out,
    ids, tapers, aperture, jitter, traces, table,
    spec, strips, zsend, zrecv, base, state, turn, green, pick, place, lsend, lrecv, asend, arecv, bsend, brecv,
    load_sem, zsend_sem, zrecv_sem, label_sem, asend_sem, arecv_sem, bsend_sem, brecv_sem, ready,
):
    me = lax.axis_index("shot")
    tile = lax.axis_index("recv")
    my_y, my_x = me >> 2, me & 3
    barrier = pltpu.get_barrier_semaphore()

    def shot_peer(offset):
        return ((my_y + offset[0]) & 3) * 4 + ((my_x + offset[1]) & 3)

    def at_shot(peer):
        return {"device_id": {"shot": peer}, "device_id_type": MESH}

    def at_recv(step):
        return {"device_id": {"recv": tile + step}, "device_id_type": MESH}

    def exists(step):
        return (tile + step >= 0) & (tile + step < tiles)

    for offset in OFFSETS:
        pl.semaphore_signal(barrier, inc=1, **at_shot(shot_peer(offset)))
    def slow(reader):
        return (reader >= 4) & (reader < 11) & (reader % 2 == 0)

    peers = jnp.int32(len(OFFSETS))
    for step in DIRS:
        heard = exists(step) & jnp.logical_not(slow(tile + 3)) if step == 3 else exists(step)
        peers = peers + heard.astype(I32)

        @pl.when(exists(step) & jnp.logical_not(slow(tile)) if step == -3 else exists(step))
        def _():
            pl.semaphore_signal(barrier, inc=1, **at_recv(step))

    loads = [
        pltpu.make_async_copy(ids_in, ids, load_sem.at[0]),
        pltpu.make_async_copy(tapers_in, tapers, load_sem.at[1]),
        pltpu.make_async_copy(aperture_in, aperture, load_sem.at[2]),
        pltpu.make_async_copy(jitter_in, jitter, load_sem.at[3]),
        pltpu.make_async_copy(table_in, table, load_sem.at[4]),
    ]
    part = SRC // LOADS
    for p in range(LOADS):
        rows = pl.ds(p * part, part)
        loads.append(pltpu.make_async_copy(traces_in.at[rows], traces.at[rows], load_sem.at[5 + p]))
    for load in loads:
        load.start()

    for load in loads[:5]:
        load.wait()

    taper = jnp.zeros((SRC, TILE), I32)
    for a in range(SRC):
        taper = jnp.where(iota((SRC, TILE), 0) == a, tapers[a], taper)
    ramp = (iota((SRC, TILE), 1) - taper * 16).astype(F32) * (1.0 / 16.0)
    ramp = sine(jnp.clip(ramp, 0.0, 1.0) * (0.5 * math.pi))
    chosen = ramp * ramp

    lane = iota((8, TILE), 1)
    owner = jnp.zeros((8, TILE), I32)
    for a in range(SRC):
        owner = jnp.where((lane & 15) == a, ids[a] >> 4, owner)
    rank = jnp.zeros((8, TILE), I32)
    for a in range(SRC):
        rank = rank + ((owner == (ids[a] >> 4)) & ((lane & 15) > a)).astype(I32)
    shape = (SRC * 16, TILE)
    row, lane = iota(shape, 0), iota(shape, 1)
    same = (owner[:1] == (row >> 4)) & (rank[:1] == (row & 1)) & (((row >> 1) & 7) == (lane >> 4))
    pick[...] = same.astype(F32).astype(BF16)

    for a in range(SRC):
        if a % part == 0:
            loads[5 + a // part].wait()
        windowed = (traces[a].astype(F32) * chosen[a : a + 1, :]).astype(BF16)
        spec[pl.ds(a, 2 * FREQS, stride=SRC), :] = lax.dot_general(
            table[...], windowed, (((1,), (1,)), ((), ())), preferred_element_type=F32
        )

    wants = []
    for step in DIRS:
        reader = lax.rem(tile + step + tiles, tiles)
        want = jnp.int32(0)
        for g in range(APER):
            entry = aperture[g, reader]
            want = jnp.where((entry >= 0) & ((entry >> 2) == tile), entry & 3, want)
        wants.append(want)

    def split_strips(m, q, panel):
        quad = m * PER + q
        strips[quad] = panel.T.astype(BF16).reshape(STRIPS, STRIP, TILE)
        pieces = [strips[quad, s] for s in range(STRIPS)]
        for k in range(len(DIRS)):
            zsend[m, k, q] = choose(wants[k], range(STRIPS), pieces)

    def spec_panel(m, q):
        return spec[pl.ds(pl.multiple_of((m * PER + q) * TILE, TILE), TILE), :]

    def send_strips(first, count, group, which):
        chunks = pl.ds(first, count)
        for k in which:
            step = DIRS[k]

            @pl.when(exists(step))
            def _():
                pltpu.make_async_remote_copy(
                    zsend.at[chunks, k],
                    zrecv.at[chunks, len(DIRS) - 1 - k],
                    zsend_sem.at[k],
                    zrecv_sem.at[group, len(DIRS) - 1 - k],
                    **at_recv(step),
                ).start()

    def wait_strips(first, count, group):
        chunks = pl.ds(first, count)
        for k, step in enumerate(DIRS):

            @pl.when(exists(step))
            def _():
                pltpu.make_async_copy(zrecv.at[chunks, k], zrecv.at[chunks, k], zrecv_sem.at[group, k]).wait()

    def lay_rows(panels):
        slots = jnp.dot(pick[...], jnp.concatenate(panels, axis=1), preferred_element_type=F32).astype(BF16)
        return [slots[:, TILE * q : TILE * (q + 1)].reshape(SRC, 16, TILE) for q in range(PER)]

    def send_rows(first, count, group):
        chunks = pl.ds(first, count)
        for offset in OFFSETS:
            peer = shot_peer(offset)
            pltpu.make_async_remote_copy(
                asend.at[chunks, peer], arecv.at[chunks, me], asend_sem, arecv_sem.at[group], **at_shot(peer)
            ).start()

    def placed_rows(blocks):
        rows = jnp.dot(place[...], jnp.concatenate(blocks, axis=1), preferred_element_type=F32)
        return [rows[:, TILE * q : TILE * (q + 1)] for q in range(PER)]

    def lay_late(late):
        blocks = lay_rows([spec_panel(EARLY + late, q).astype(BF16) for q in range(PER)])
        for q in range(PER):
            first = 16 * (late * PER + q)
            bsend[:, first : first + 16, :] = blocks[q]

    for q in range(PER):
        split_strips(0, q, spec_panel(0, q))
    for late in range(LATE) if EAGER else ():
        lay_late(late)
    pl.semaphore_wait(barrier, peers)

    @pl.when(exists(-3) & slow(tile))
    def _():
        pl.semaphore_signal(ready, inc=1, **at_recv(-3))

    def send_near(group):
        first, count = GROUPS[group]
        send_strips(first, count, group, NEAR)

        @pl.when(jnp.logical_not(slow(tile + 3)))
        def _():
            send_strips(first, count, group, FAR)

    send_near(0)
    for late in range(LATE) if not EAGER else ():
        lay_late(late)
    for offset in OFFSETS:
        peer = shot_peer(offset)
        pltpu.make_async_remote_copy(bsend.at[peer], brecv.at[me], bsend_sem, brecv_sem, **at_shot(peer)).start()
    brecv[me] = bsend[me]
    for group in range(1, len(GROUPS)):
        first, count = GROUPS[group]
        for m in range(first, first + count):
            for q in range(PER):
                split_strips(m, q, spec_panel(m, q))
        send_near(group)

    row, lane = iota((SRC, TILE), 0), iota((SRC, TILE), 1)
    label = jnp.full((SRC, TILE), -1, I32)
    count = jnp.zeros((SRC, TILE), I32)
    for a in range(SRC):
        hit = row == (ids[a] >> 4)
        label = jnp.where(hit & (count == (lane & 1)), ids[a] & 15, label)
        count = count + hit.astype(I32)
    for t in range(SRC):
        lsend[t] = label[t : t + 1, :]
    lrecv[me] = lsend[me]
    for offset in OFFSETS:
        peer = shot_peer(offset)
        pltpu.make_async_remote_copy(
            lsend.at[peer], lrecv.at[me], label_sem.at[0], label_sem.at[1], **at_shot(peer)
        ).start()

    row, lane = iota((STRIP, TILE), 0), iota((STRIP, TILE), 1)
    here = pl.ds(pl.multiple_of(tile * TILE, TILE), TILE)
    local_x = (tile * TILE + lane).astype(F32) + 0.4 * jitter[0:1, here]
    local_y = 3.0 * jitter[1:2, here]
    near = (0,) + DIRS
    jitters = []
    for step in near:
        there = lax.rem(tile + step + tiles, tiles)
        jitters.append(jitter[:, pl.ds(pl.multiple_of(there * TILE, TILE), TILE)])
    sources = []
    for g in range(APER):
        entry = aperture[g, tile]
        live = (entry >= 0).astype(F32)
        sources.append(jnp.where(entry >= 0, (entry >> 2) - tile, 0))
        strip = jnp.maximum(entry, 0)
        there = choose(sources[g], near, jitters)
        mask = lane == row + (strip & 3) * STRIP
        strip_x = jnp.sum(jnp.where(mask, there[0:1], 0.0), axis=1, keepdims=True)
        strip_y = jnp.sum(jnp.where(mask, there[1:2], 0.0), axis=1, keepdims=True)
        dx = (strip * STRIP + row).astype(F32) + 0.4 * strip_x - local_x
        dy = 3.0 * strip_y - local_y
        square = dx * dx + dy * dy
        cut = jnp.minimum(jnp.sqrt(square) * (1.0 / ((HALF + 1) * TILE)), 1.0)
        amp = cosine(cut * (0.5 * math.pi)) * (live / math.sqrt(APER * STRIP))
        turns = jnp.sqrt(square + 64.0) * (0.5 / 32.0)
        quarter = (turns - jnp.floor(turns + 0.5)) * math.pi
        sin_q, cos_q = sine(quarter), cosine(quarter)
        half = (1.0 - 2.0 * sin_q * sin_q, 2.0 * sin_q * cos_q)
        whole = plus(half, half)
        now = half
        for j in range(4):
            base[g, j, 0] = amp * now[0]
            base[g, j, 1] = amp * now[1]
            if j < 3:
                now = plus(now, whole)
        two = plus(whole, whole)
        four = plus(two, two)
        eight = plus(four, four)
        state[g, 0], state[g, 1] = four
        turn[g, 0], turn[g, 1] = eight

    @pl.when(exists(3) & slow(tile + 3))
    def _():
        pl.semaphore_wait(ready, 1)
        for group, (first, count) in enumerate(GROUPS):
            send_strips(first, count, group, FAR)

    own_strip = aperture[0, tile] & 3

    def make_green(m, carry):
        for g in range(APER):
            rows = pl.ds(g * STRIP, STRIP)
            cos_a, sin_a = state[g, 0], state[g, 1]
            for j in range(4):
                cos_b, sin_b = base[g, j, 0], base[g, j, 1]
                cc, ss, sc, cs = cos_a * cos_b, sin_a * sin_b, sin_a * cos_b, cos_a * sin_b
                green[m, 4 + j, rows, 0:TILE] = (cc - ss).astype(BF16)
                green[m, 4 + j, rows, TILE : 2 * TILE] = (-sc - cs).astype(BF16)
                green[m, 3 - j, rows, 0:TILE] = (cc + ss).astype(BF16)
                green[m, 3 - j, rows, TILE : 2 * TILE] = (cs - sc).astype(BF16)
            state[g, 0], state[g, 1] = plus((cos_a, sin_a), (turn[g, 0], turn[g, 1]))
        return carry

    lax.fori_loop(0, EARLY, make_green, 0)

    def product(m):
        panels = []
        for q in range(PER):
            own = choose(own_strip, range(STRIPS), [strips[m * PER + q, s] for s in range(STRIPS)])
            pieces = [own]
            options = [own] + [zrecv[m, k, q] for k in range(len(DIRS))]
            for g in range(1, APER):
                pieces.append(choose(sources[g], near, options))
            panel = jnp.concatenate(pieces, axis=0).T
            parts = []
            for f in range(4):
                both = jnp.dot(
                    panel[2 * SRC * f : 2 * SRC * (f + 1)], green[m, 4 * q + f], preferred_element_type=F32
                )
                parts.append(both[:SRC, :TILE] - both[SRC:, TILE:])
                parts.append(both[:SRC, TILE:] + both[SRC:, :TILE])
            panels.append(jnp.concatenate(parts, axis=0).astype(BF16))
        return panels

    def store(m, panels):
        for q in range(PER):
            panel = panels[q].astype(BF16).reshape(4, 2, SRC, TILE)
            for c in range(2):
                out[c, pl.ds((m * PER + q) * 4, 4)] = panel[:, c]

    def early(m, carry):
        blocks = lay_rows(product(m))
        for q in range(PER):
            asend[m, :, 16 * q : 16 * (q + 1), :] = blocks[q]
        arecv[m, me] = asend[m, me]
        return carry

    def early_group(group):
        first, count = GROUPS[group]
        wait_strips(first, count, group)
        lax.fori_loop(first, first + count, early, 0)
        send_rows(first, count, group)

    for group in range(SHIFT):
        early_group(group)

    most = lrecv.at[pl.ds(0, SRC - 1)]
    pltpu.make_async_copy(most, most, label_sem.at[1]).wait()
    row, lane = iota((TILE, TILE), 0), iota((TILE, TILE), 1)
    for h in range(2):
        label = jnp.zeros((1, TILE), I32)
        for j in range(8):
            label = jnp.where(iota((1, TILE), 1) >> 4 == j, lrecv[8 * h + j], label)
        same = (label == (row & 15)) & (((lane >> 1) & 7) == (row >> 4))
        place[:, TILE * h : TILE * (h + 1)] = same.astype(F32).astype(BF16)

    most = brecv.at[pl.ds(0, SRC - 1)]
    pltpu.make_async_copy(most, most, brecv_sem).wait()

    def relay(m, carry):
        first = pl.multiple_of((m - EARLY) * PER * 16, PER * 16)
        rows = brecv[:, pl.ds(first, PER * 16), :]
        rows = placed_rows([rows[:, 16 * q : 16 * (q + 1)].reshape(SRC * 16, TILE) for q in range(PER)])
        for q in range(PER):
            split_strips(m, q, rows[q])
        send_strips(m, 1, m - EARLY + len(GROUPS), ALL)
        return carry

    lax.fori_loop(EARLY, CHUNKS, relay, 0)
    for group in range(SHIFT, len(GROUPS)):
        early_group(group)

    lax.fori_loop(EARLY, CHUNKS, make_green, 0)

    def finish(m, carry):
        store(m, placed_rows([arecv[m, :, 16 * q : 16 * (q + 1), :].reshape(SRC * 16, TILE) for q in range(PER)]))
        return carry

    def finish_group(group):
        first, count = GROUPS[group]
        most = arecv.at[pl.ds(first, count), pl.ds(0, SRC - 1)]
        pltpu.make_async_copy(most, most, arecv_sem.at[group]).wait()
        lax.fori_loop(first, first + count, finish, 0)

    for group in range(HOLD):
        finish_group(group)

    def late(m, carry):
        wait_strips(m, 1, m - EARLY + len(GROUPS))
        store(m, product(m))
        return carry

    lax.fori_loop(EARLY, CHUNKS, late, 0)
    for group in range(HOLD, len(GROUPS)):
        finish_group(group)

    for k, step in enumerate(DIRS):

        @pl.when(exists(step))
        def _():
            pltpu.make_async_copy(zsend.at[:, k], zsend.at[:, k], zsend_sem.at[k]).wait()

    most = lsend.at[pl.ds(0, SRC - 1)]
    pltpu.make_async_copy(most, most, label_sem.at[0]).wait()
    most = asend.at[:, pl.ds(0, SRC - 1)]
    pltpu.make_async_copy(most, most, asend_sem).wait()
    most = bsend.at[pl.ds(0, SRC - 1)]
    pltpu.make_async_copy(most, most, bsend_sem).wait()


def dft_table():
    samples = np.arange(TILE)[None, :]
    bins = np.arange(FREQS)[:, None]
    angle = np.pi * ((2 * bins + 1) * samples % (2 * TILE)) / TILE
    values = np.stack([np.cos(angle), -np.sin(angle)], axis=1) / math.sqrt(TILE)
    return values.reshape(2 * FREQS, TILE)


def local(tiles, traces, source_ids, taper_ids, recv_jitter, aperture):
    hbm = pl.BlockSpec(memory_space=pltpu.HBM)
    table = jnp.asarray(dft_table(), BF16)
    dirs = len(DIRS)
    return pl.pallas_call(
        functools.partial(kernel, tiles),
        out_shape=pltpu.VMEM((2, FREQS, SRC, TILE), BF16),
        in_specs=[hbm] * 6,
        out_specs=pl.BlockSpec(memory_space=pltpu.VMEM),
        scratch_shapes=[
            pltpu.SMEM((SRC,), I32),
            pltpu.SMEM((SRC,), I32),
            pltpu.SMEM((APER, tiles), I32),
            pltpu.VMEM(recv_jitter.shape, F32),
            pltpu.VMEM(traces.shape, BF16),
            pltpu.VMEM(table.shape, BF16),
            pltpu.VMEM((2 * FREQS * SRC, TILE), F32),
            pltpu.VMEM((QUADS, STRIPS, STRIP, TILE), BF16),
            pltpu.VMEM((CHUNKS, dirs, PER, STRIP, TILE), BF16),
            pltpu.VMEM((CHUNKS, dirs, PER, STRIP, TILE), BF16),
            pltpu.VMEM((APER, 4, 2, STRIP, TILE), F32),
            pltpu.VMEM((APER, 2, STRIP, TILE), F32),
            pltpu.VMEM((APER, 2, STRIP, TILE), F32),
            pltpu.VMEM((CHUNKS, 8, APER * STRIP, 2 * TILE), BF16),
            pltpu.VMEM((SRC * 16, TILE), BF16),
            pltpu.VMEM((TILE, SRC * 16), BF16),
            pltpu.VMEM((SRC, 1, TILE), I32),
            pltpu.VMEM((SRC, 1, TILE), I32),
            pltpu.VMEM((EARLY, SRC, 16 * PER, TILE), BF16),
            pltpu.VMEM((EARLY, SRC, 16 * PER, TILE), BF16),
            pltpu.VMEM((SRC, LATE * 16 * PER, TILE), BF16),
            pltpu.VMEM((SRC, LATE * 16 * PER, TILE), BF16),
            pltpu.SemaphoreType.DMA((5 + LOADS,)),
            pltpu.SemaphoreType.DMA((dirs,)),
            pltpu.SemaphoreType.DMA((len(GROUPS) + LATE, dirs)),
            pltpu.SemaphoreType.DMA((2,)),
            pltpu.SemaphoreType.DMA,
            pltpu.SemaphoreType.DMA((len(GROUPS),)),
            pltpu.SemaphoreType.DMA,
            pltpu.SemaphoreType.DMA,
            pltpu.SemaphoreType.REGULAR,
        ],
        compiler_params=pltpu.CompilerParams(
            collective_id=0, has_side_effects=True, vmem_limit_bytes=62 * 1024 * 1024
        ),
    )(source_ids, taper_ids, aperture.T, recv_jitter, traces, table)


def solution(mesh):
    placed = (P("shot", "recv", None), P("shot"), P("shot"), P(), P())
    return jax.shard_map(
        functools.partial(local, mesh.shape["recv"]),
        mesh=mesh,
        in_specs=placed,
        out_specs=P(None, None, "shot", "recv"),
        check_vma=False,
    )
```

```python
import functools
import math

import jax
import jax.numpy as jnp
import numpy as np
from jax import lax
from jax.experimental import pallas as pl
from jax.experimental.pallas import tpu as pltpu
from jax.sharding import PartitionSpec as P

FREQS = 64
STRIPS = 4
APER = 5
HALF = 3
SRC = 16
TILE = 128
STRIP = 32
SLOTS = 2
QUADS = FREQS // 4
PER = 2
CHUNKS = QUADS // PER
LATE = 3
EARLY = CHUNKS - LATE
LOADS = 4
HOLD = 3
SHIFT = 3
EAGER = True
OFFSETS = sorted(
    ((dy, dx) for dy in range(4) for dx in range(4) if dy or dx),
    key=lambda o: -(min(o[0], 4 - o[0]) + min(o[1], 4 - o[1])),
)
DIRS = (-3, -2, -1, 1, 2, 3)
GROUPS = ((0, 1), (1, 1), (2, 1), (3, 1), (4, 1))
ALL, NEAR, FAR = range(6), range(5), range(5, 6)
MESH = pl.DeviceIdType.MESH
F32, BF16, I32 = jnp.float32, jnp.bfloat16, jnp.int32


def sine(x):
    z = x * x
    total = jnp.full_like(x, 1.0 / 6227020800.0)
    for term in (-1.0 / 39916800.0, 1.0 / 362880.0, -1.0 / 5040.0, 1.0 / 120.0, -1.0 / 6.0, 1.0):
        total = total * z + term
    return total * x


def cosine(x):
    z = x * x
    total = jnp.full_like(x, 1.0 / 479001600.0)
    for term in (-1.0 / 3628800.0, 1.0 / 40320.0, -1.0 / 720.0, 1.0 / 24.0, -0.5, 1.0):
        total = total * z + term
    return total


def iota(shape, dim):
    return lax.broadcasted_iota(I32, shape, dim)


def choose(which, options, values):
    chosen = values[0]
    for option, value in zip(options[1:], values[1:]):
        chosen = jnp.where(which == option, value, chosen)
    return chosen


def plus(one, two):
    return one[0] * two[0] - one[1] * two[1], one[1] * two[0] + one[0] * two[1]


def kernel(
    tiles, ids_in, tapers_in, aperture_in, jitter_in, traces_in, table_in, out,
    ids, tapers, aperture, jitter, traces, table,
    spec, strips, zsend, zrecv, base, state, turn, green, pick, place, lsend, lrecv, asend, arecv, bsend, brecv,
    load_sem, zsend_sem, zrecv_sem, label_sem, asend_sem, arecv_sem, bsend_sem, brecv_sem, ready,
):
    me = lax.axis_index("shot")
    tile = lax.axis_index("recv")
    my_y, my_x = me >> 2, me & 3
    barrier = pltpu.get_barrier_semaphore()

    def shot_peer(offset):
        return ((my_y + offset[0]) & 3) * 4 + ((my_x + offset[1]) & 3)

    def at_shot(peer):
        return {"device_id": {"shot": peer}, "device_id_type": MESH}

    def at_recv(step):
        return {"device_id": {"recv": tile + step}, "device_id_type": MESH}

    def exists(step):
        return (tile + step >= 0) & (tile + step < tiles)

    for offset in OFFSETS:
        pl.semaphore_signal(barrier, inc=1, **at_shot(shot_peer(offset)))
    def slow(reader):
        return (reader >= 4) & (reader < 11)

    peers = jnp.int32(len(OFFSETS))
    for step in DIRS:
        heard = exists(step) & jnp.logical_not(slow(tile + 3)) if step == 3 else exists(step)
        peers = peers + heard.astype(I32)

        @pl.when(exists(step) & jnp.logical_not(slow(tile)) if step == -3 else exists(step))
        def _():
            pl.semaphore_signal(barrier, inc=1, **at_recv(step))

    loads = [
        pltpu.make_async_copy(ids_in, ids, load_sem.at[0]),
        pltpu.make_async_copy(tapers_in, tapers, load_sem.at[1]),
        pltpu.make_async_copy(aperture_in, aperture, load_sem.at[2]),
        pltpu.make_async_copy(jitter_in, jitter, load_sem.at[3]),
        pltpu.make_async_copy(table_in, table, load_sem.at[4]),
    ]
    part = SRC // LOADS
    for p in range(LOADS):
        rows = pl.ds(p * part, part)
        loads.append(pltpu.make_async_copy(traces_in.at[rows], traces.at[rows], load_sem.at[5 + p]))
    for load in loads:
        load.start()

    for load in loads[:5]:
        load.wait()

    taper = jnp.zeros((SRC, TILE), I32)
    for a in range(SRC):
        taper = jnp.where(iota((SRC, TILE), 0) == a, tapers[a], taper)
    ramp = (iota((SRC, TILE), 1) - taper * 16).astype(F32) * (1.0 / 16.0)
    ramp = sine(jnp.clip(ramp, 0.0, 1.0) * (0.5 * math.pi))
    chosen = ramp * ramp

    lane = iota((8, TILE), 1)
    owner = jnp.zeros((8, TILE), I32)
    for a in range(SRC):
        owner = jnp.where((lane & 15) == a, ids[a] >> 4, owner)
    rank = jnp.zeros((8, TILE), I32)
    for a in range(SRC):
        rank = rank + ((owner == (ids[a] >> 4)) & ((lane & 15) > a)).astype(I32)
    shape = (SRC * 16, TILE)
    row, lane = iota(shape, 0), iota(shape, 1)
    same = (owner[:1] == (row >> 4)) & (rank[:1] == (row & 1)) & (((row >> 1) & 7) == (lane >> 4))
    pick[...] = same.astype(F32).astype(BF16)

    for a in range(0, SRC, 2):
        if a % part == 0:
            loads[5 + a // part].wait()
        both = [(traces[b].astype(F32) * chosen[b : b + 1, :]).astype(BF16) for b in (a, a + 1)]
        spectra = lax.dot_general(
            table[...], jnp.concatenate(both, axis=0), (((1,), (1,)), ((), ())), preferred_element_type=F32
        )
        for b in range(2):
            spec[pl.ds(a + b, 2 * FREQS, stride=SRC), :] = spectra[:, TILE * b : TILE * (b + 1)]

    wants = []
    for step in DIRS:
        reader = lax.rem(tile + step + tiles, tiles)
        want = jnp.int32(0)
        for g in range(APER):
            entry = aperture[g, reader]
            want = jnp.where((entry >= 0) & ((entry >> 2) == tile), entry & 3, want)
        wants.append(want)

    def split_strips(m, q, panel):
        quad = m * PER + q
        strips[quad] = panel.T.astype(BF16).reshape(STRIPS, STRIP, TILE)
        pieces = [strips[quad, s] for s in range(STRIPS)]
        for k in range(len(DIRS)):
            zsend[m, k, q] = choose(wants[k], range(STRIPS), pieces)

    def spec_panel(m, q):
        return spec[pl.ds(pl.multiple_of((m * PER + q) * TILE, TILE), TILE), :]

    def send_strips(first, count, group, which):
        chunks = pl.ds(first, count)
        for k in which:
            step = DIRS[k]

            @pl.when(exists(step))
            def _():
                pltpu.make_async_remote_copy(
                    zsend.at[chunks, k],
                    zrecv.at[chunks, len(DIRS) - 1 - k],
                    zsend_sem.at[k],
                    zrecv_sem.at[group, len(DIRS) - 1 - k],
                    **at_recv(step),
                ).start()

    def wait_strips(first, count, group):
        chunks = pl.ds(first, count)
        for k, step in enumerate(DIRS):

            @pl.when(exists(step))
            def _():
                pltpu.make_async_copy(zrecv.at[chunks, k], zrecv.at[chunks, k], zrecv_sem.at[group, k]).wait()

    def lay_rows(panels):
        slots = jnp.dot(pick[...], jnp.concatenate(panels, axis=1), preferred_element_type=F32).astype(BF16)
        return [slots[:, TILE * q : TILE * (q + 1)].reshape(SRC, 16, TILE) for q in range(PER)]

    def send_rows(first, count, group):
        chunks = pl.ds(first, count)
        for offset in OFFSETS:
            peer = shot_peer(offset)
            pltpu.make_async_remote_copy(
                asend.at[chunks, peer], arecv.at[chunks, me], asend_sem, arecv_sem.at[group], **at_shot(peer)
            ).start()

    def placed_rows(blocks):
        rows = jnp.dot(place[...], jnp.concatenate(blocks, axis=1), preferred_element_type=F32)
        return [rows[:, TILE * q : TILE * (q + 1)] for q in range(PER)]

    def lay_late(late):
        blocks = lay_rows([spec_panel(EARLY + late, q).astype(BF16) for q in range(PER)])
        for q in range(PER):
            first = 16 * (late * PER + q)
            bsend[:, first : first + 16, :] = blocks[q]

    for q in range(PER):
        split_strips(0, q, spec_panel(0, q))
    for late in range(LATE) if EAGER else ():
        lay_late(late)
    pl.semaphore_wait(barrier, peers)

    @pl.when(exists(-3) & slow(tile))
    def _():
        pl.semaphore_signal(ready, inc=1, **at_recv(-3))

    def send_near(group):
        first, count = GROUPS[group]
        send_strips(first, count, group, NEAR)

        @pl.when(jnp.logical_not(slow(tile + 3)))
        def _():
            send_strips(first, count, group, FAR)

    send_near(0)
    for late in range(LATE) if not EAGER else ():
        lay_late(late)
    for offset in OFFSETS:
        peer = shot_peer(offset)
        pltpu.make_async_remote_copy(bsend.at[peer], brecv.at[me], bsend_sem, brecv_sem, **at_shot(peer)).start()
    brecv[me] = bsend[me]
    for group in range(1, len(GROUPS)):
        first, count = GROUPS[group]
        for m in range(first, first + count):
            for q in range(PER):
                split_strips(m, q, spec_panel(m, q))
        send_near(group)

    row, lane = iota((SRC, TILE), 0), iota((SRC, TILE), 1)
    label = jnp.full((SRC, TILE), -1, I32)
    count = jnp.zeros((SRC, TILE), I32)
    for a in range(SRC):
        hit = row == (ids[a] >> 4)
        label = jnp.where(hit & (count == (lane & 1)), ids[a] & 15, label)
        count = count + hit.astype(I32)
    for t in range(SRC):
        lsend[t] = label[t : t + 1, :]
    lrecv[me] = lsend[me]
    for offset in OFFSETS:
        peer = shot_peer(offset)
        pltpu.make_async_remote_copy(
            lsend.at[peer], lrecv.at[me], label_sem.at[0], label_sem.at[1], **at_shot(peer)
        ).start()

    row, lane = iota((STRIP, TILE), 0), iota((STRIP, TILE), 1)
    here = pl.ds(pl.multiple_of(tile * TILE, TILE), TILE)
    local_x = (tile * TILE + lane).astype(F32) + 0.4 * jitter[0:1, here]
    local_y = 3.0 * jitter[1:2, here]
    near = (0,) + DIRS
    jitters = []
    for step in near:
        there = lax.rem(tile + step + tiles, tiles)
        jitters.append(jitter[:, pl.ds(pl.multiple_of(there * TILE, TILE), TILE)])
    sources = []
    for g in range(APER):
        entry = aperture[g, tile]
        live = (entry >= 0).astype(F32)
        sources.append(jnp.where(entry >= 0, (entry >> 2) - tile, 0))
        strip = jnp.maximum(entry, 0)
        there = choose(sources[g], near, jitters)
        mask = lane == row + (strip & 3) * STRIP
        strip_x = jnp.sum(jnp.where(mask, there[0:1], 0.0), axis=1, keepdims=True)
        strip_y = jnp.sum(jnp.where(mask, there[1:2], 0.0), axis=1, keepdims=True)
        dx = (strip * STRIP + row).astype(F32) + 0.4 * strip_x - local_x
        dy = 3.0 * strip_y - local_y
        square = dx * dx + dy * dy
        cut = jnp.minimum(jnp.sqrt(square) * (1.0 / ((HALF + 1) * TILE)), 1.0)
        amp = cosine(cut * (0.5 * math.pi)) * (live / math.sqrt(APER * STRIP))
        turns = jnp.sqrt(square + 64.0) * (0.5 / 32.0)
        quarter = (turns - jnp.floor(turns + 0.5)) * math.pi
        sin_q, cos_q = sine(quarter), cosine(quarter)
        half = (1.0 - 2.0 * sin_q * sin_q, 2.0 * sin_q * cos_q)
        whole = plus(half, half)
        now = half
        for j in range(4):
            base[g, j, 0] = amp * now[0]
            base[g, j, 1] = amp * now[1]
            if j < 3:
                now = plus(now, whole)
        two = plus(whole, whole)
        four = plus(two, two)
        eight = plus(four, four)
        state[g, 0], state[g, 1] = four
        turn[g, 0], turn[g, 1] = eight

    @pl.when(exists(3) & slow(tile + 3))
    def _():
        pl.semaphore_wait(ready, 1)
        for group, (first, count) in enumerate(GROUPS):
            send_strips(first, count, group, FAR)

    own_strip = aperture[0, tile] & 3

    def make_green(m, carry):
        for g in range(APER):
            rows = pl.ds(g * STRIP, STRIP)
            cos_a, sin_a = state[g, 0], state[g, 1]
            for j in range(4):
                cos_b, sin_b = base[g, j, 0], base[g, j, 1]
                cc, ss, sc, cs = cos_a * cos_b, sin_a * sin_b, sin_a * cos_b, cos_a * sin_b
                green[m, 4 + j, rows, 0:TILE] = (cc - ss).astype(BF16)
                green[m, 4 + j, rows, TILE : 2 * TILE] = (-sc - cs).astype(BF16)
                green[m, 3 - j, rows, 0:TILE] = (cc + ss).astype(BF16)
                green[m, 3 - j, rows, TILE : 2 * TILE] = (cs - sc).astype(BF16)
            state[g, 0], state[g, 1] = plus((cos_a, sin_a), (turn[g, 0], turn[g, 1]))
        return carry

    lax.fori_loop(0, EARLY, make_green, 0)

    def product(m):
        panels = []
        for q in range(PER):
            own = choose(own_strip, range(STRIPS), [strips[m * PER + q, s] for s in range(STRIPS)])
            pieces = [own]
            options = [own] + [zrecv[m, k, q] for k in range(len(DIRS))]
            for g in range(1, APER):
                pieces.append(choose(sources[g], near, options))
            panel = jnp.concatenate(pieces, axis=0).T
            parts = []
            for f in range(4):
                both = jnp.dot(
                    panel[2 * SRC * f : 2 * SRC * (f + 1)], green[m, 4 * q + f], preferred_element_type=F32
                )
                parts.append(both[:SRC, :TILE] - both[SRC:, TILE:])
                parts.append(both[:SRC, TILE:] + both[SRC:, :TILE])
            panels.append(jnp.concatenate(parts, axis=0).astype(BF16))
        return panels

    def store(m, panels):
        for q in range(PER):
            panel = panels[q].astype(BF16).reshape(4, 2, SRC, TILE)
            for c in range(2):
                out[c, pl.ds((m * PER + q) * 4, 4)] = panel[:, c]

    def early(m, carry):
        blocks = lay_rows(product(m))
        for q in range(PER):
            asend[m, :, 16 * q : 16 * (q + 1), :] = blocks[q]
        arecv[m, me] = asend[m, me]
        return carry

    def early_group(group):
        first, count = GROUPS[group]
        wait_strips(first, count, group)
        lax.fori_loop(first, first + count, early, 0)
        send_rows(first, count, group)

    for group in range(SHIFT):
        early_group(group)

    most = lrecv.at[pl.ds(0, SRC - 1)]
    pltpu.make_async_copy(most, most, label_sem.at[1]).wait()
    row, lane = iota((TILE, TILE), 0), iota((TILE, TILE), 1)
    for h in range(2):
        label = jnp.zeros((1, TILE), I32)
        for j in range(8):
            label = jnp.where(iota((1, TILE), 1) >> 4 == j, lrecv[8 * h + j], label)
        same = (label == (row & 15)) & (((lane >> 1) & 7) == (row >> 4))
        place[:, TILE * h : TILE * (h + 1)] = same.astype(F32).astype(BF16)

    most = brecv.at[pl.ds(0, SRC - 1)]
    pltpu.make_async_copy(most, most, brecv_sem).wait()

    def relay(m, carry):
        first = pl.multiple_of((m - EARLY) * PER * 16, PER * 16)
        rows = brecv[:, pl.ds(first, PER * 16), :]
        rows = placed_rows([rows[:, 16 * q : 16 * (q + 1)].reshape(SRC * 16, TILE) for q in range(PER)])
        for q in range(PER):
            split_strips(m, q, rows[q])
        send_strips(m, 1, m - EARLY + len(GROUPS), ALL)
        return carry

    lax.fori_loop(EARLY, CHUNKS, relay, 0)
    for group in range(SHIFT, len(GROUPS)):
        early_group(group)

    lax.fori_loop(EARLY, CHUNKS, make_green, 0)

    def finish(m, carry):
        store(m, placed_rows([arecv[m, :, 16 * q : 16 * (q + 1), :].reshape(SRC * 16, TILE) for q in range(PER)]))
        return carry

    def finish_group(group):
        first, count = GROUPS[group]
        most = arecv.at[pl.ds(first, count), pl.ds(0, SRC - 1)]
        pltpu.make_async_copy(most, most, arecv_sem.at[group]).wait()
        lax.fori_loop(first, first + count, finish, 0)

    for group in range(HOLD):
        finish_group(group)

    def late(m, carry):
        wait_strips(m, 1, m - EARLY + len(GROUPS))
        store(m, product(m))
        return carry

    lax.fori_loop(EARLY, CHUNKS, late, 0)
    for group in range(HOLD, len(GROUPS)):
        finish_group(group)

    for k, step in enumerate(DIRS):

        @pl.when(exists(step))
        def _():
            pltpu.make_async_copy(zsend.at[:, k], zsend.at[:, k], zsend_sem.at[k]).wait()

    most = lsend.at[pl.ds(0, SRC - 1)]
    pltpu.make_async_copy(most, most, label_sem.at[0]).wait()
    most = asend.at[:, pl.ds(0, SRC - 1)]
    pltpu.make_async_copy(most, most, asend_sem).wait()
    most = bsend.at[pl.ds(0, SRC - 1)]
    pltpu.make_async_copy(most, most, bsend_sem).wait()


def dft_table():
    samples = np.arange(TILE)[None, :]
    bins = np.arange(FREQS)[:, None]
    angle = np.pi * ((2 * bins + 1) * samples % (2 * TILE)) / TILE
    values = np.stack([np.cos(angle), -np.sin(angle)], axis=1) / math.sqrt(TILE)
    return values.reshape(2 * FREQS, TILE)


def local(tiles, traces, source_ids, taper_ids, recv_jitter, aperture):
    hbm = pl.BlockSpec(memory_space=pltpu.HBM)
    table = jnp.asarray(dft_table(), BF16)
    dirs = len(DIRS)
    return pl.pallas_call(
        functools.partial(kernel, tiles),
        out_shape=pltpu.VMEM((2, FREQS, SRC, TILE), BF16),
        in_specs=[hbm] * 6,
        out_specs=pl.BlockSpec(memory_space=pltpu.VMEM),
        scratch_shapes=[
            pltpu.SMEM((SRC,), I32),
            pltpu.SMEM((SRC,), I32),
            pltpu.SMEM((APER, tiles), I32),
            pltpu.VMEM(recv_jitter.shape, F32),
            pltpu.VMEM(traces.shape, BF16),
            pltpu.VMEM(table.shape, BF16),
            pltpu.VMEM((2 * FREQS * SRC, TILE), F32),
            pltpu.VMEM((QUADS, STRIPS, STRIP, TILE), BF16),
            pltpu.VMEM((CHUNKS, dirs, PER, STRIP, TILE), BF16),
            pltpu.VMEM((CHUNKS, dirs, PER, STRIP, TILE), BF16),
            pltpu.VMEM((APER, 4, 2, STRIP, TILE), F32),
            pltpu.VMEM((APER, 2, STRIP, TILE), F32),
            pltpu.VMEM((APER, 2, STRIP, TILE), F32),
            pltpu.VMEM((CHUNKS, 8, APER * STRIP, 2 * TILE), BF16),
            pltpu.VMEM((SRC * 16, TILE), BF16),
            pltpu.VMEM((TILE, SRC * 16), BF16),
            pltpu.VMEM((SRC, 1, TILE), I32),
            pltpu.VMEM((SRC, 1, TILE), I32),
            pltpu.VMEM((EARLY, SRC, 16 * PER, TILE), BF16),
            pltpu.VMEM((EARLY, SRC, 16 * PER, TILE), BF16),
            pltpu.VMEM((SRC, LATE * 16 * PER, TILE), BF16),
            pltpu.VMEM((SRC, LATE * 16 * PER, TILE), BF16),
            pltpu.SemaphoreType.DMA((5 + LOADS,)),
            pltpu.SemaphoreType.DMA((dirs,)),
            pltpu.SemaphoreType.DMA((len(GROUPS) + LATE, dirs)),
            pltpu.SemaphoreType.DMA((2,)),
            pltpu.SemaphoreType.DMA,
            pltpu.SemaphoreType.DMA((len(GROUPS),)),
            pltpu.SemaphoreType.DMA,
            pltpu.SemaphoreType.DMA,
            pltpu.SemaphoreType.REGULAR,
        ],
        compiler_params=pltpu.CompilerParams(
            collective_id=0, has_side_effects=True, vmem_limit_bytes=62 * 1024 * 1024
        ),
    )(source_ids, taper_ids, aperture.T, recv_jitter, traces, table)


def solution(mesh):
    placed = (P("shot", "recv", None), P("shot"), P("shot"), P(), P())
    return jax.shard_map(
        functools.partial(local, mesh.shape["recv"]),
        mesh=mesh,
        in_specs=placed,
        out_specs=P(None, None, "shot", "recv"),
        check_vma=False,
    )
```

```python
import functools
import math

import jax
import jax.numpy as jnp
import numpy as np
from jax import lax
from jax.experimental import pallas as pl
from jax.experimental.pallas import tpu as pltpu
from jax.sharding import PartitionSpec as P

FREQS = 64
STRIPS = 4
APER = 5
HALF = 3
SRC = 16
TILE = 128
STRIP = 32
SLOTS = 2
QUADS = FREQS // 4
PER = 2
CHUNKS = QUADS // PER
LATE = 3
EARLY = CHUNKS - LATE
LOADS = 4
HOLD = 3
SHIFT = 3
EAGER = True
OFFSETS = sorted(
    ((dy, dx) for dy in range(4) for dx in range(4) if dy or dx),
    key=lambda o: -(min(o[0], 4 - o[0]) + min(o[1], 4 - o[1])),
)
DIRS = (-3, -2, -1, 1, 2, 3)
GROUPS = ((0, 1), (1, 1), (2, 1), (3, 1), (4, 1))
ALL, NEAR, FAR = range(6), range(5), range(5, 6)
MESH = pl.DeviceIdType.MESH
F32, BF16, I32 = jnp.float32, jnp.bfloat16, jnp.int32


def sine(x):
    z = x * x
    total = jnp.full_like(x, 1.0 / 6227020800.0)
    for term in (-1.0 / 39916800.0, 1.0 / 362880.0, -1.0 / 5040.0, 1.0 / 120.0, -1.0 / 6.0, 1.0):
        total = total * z + term
    return total * x


def cosine(x):
    z = x * x
    total = jnp.full_like(x, 1.0 / 479001600.0)
    for term in (-1.0 / 3628800.0, 1.0 / 40320.0, -1.0 / 720.0, 1.0 / 24.0, -0.5, 1.0):
        total = total * z + term
    return total


def iota(shape, dim):
    return lax.broadcasted_iota(I32, shape, dim)


def choose(which, options, values):
    chosen = values[0]
    for option, value in zip(options[1:], values[1:]):
        chosen = jnp.where(which == option, value, chosen)
    return chosen


def plus(one, two):
    return one[0] * two[0] - one[1] * two[1], one[1] * two[0] + one[0] * two[1]


def kernel(
    tiles, ids_in, tapers_in, aperture_in, jitter_in, traces_in, table_in, out,
    ids, tapers, aperture, jitter, traces, table,
    spec, strips, zsend, zrecv, base, state, turn, green, pick, place, lsend, lrecv, asend, arecv, bsend, brecv,
    load_sem, zsend_sem, zrecv_sem, label_sem, asend_sem, arecv_sem, bsend_sem, brecv_sem, ready,
):
    me = lax.axis_index("shot")
    tile = lax.axis_index("recv")
    my_y, my_x = me >> 2, me & 3
    barrier = pltpu.get_barrier_semaphore()

    def shot_peer(offset):
        return ((my_y + offset[0]) & 3) * 4 + ((my_x + offset[1]) & 3)

    def at_shot(peer):
        return {"device_id": {"shot": peer}, "device_id_type": MESH}

    def at_recv(step):
        return {"device_id": {"recv": tile + step}, "device_id_type": MESH}

    def exists(step):
        return (tile + step >= 0) & (tile + step < tiles)

    for offset in OFFSETS:
        pl.semaphore_signal(barrier, inc=1, **at_shot(shot_peer(offset)))
    def slow(reader):
        return (reader >= 4) & (reader < 11)

    peers = jnp.int32(len(OFFSETS))
    for step in DIRS:
        heard = exists(step) & jnp.logical_not(slow(tile + 3)) if step == 3 else exists(step)
        peers = peers + heard.astype(I32)

        @pl.when(exists(step) & jnp.logical_not(slow(tile)) if step == -3 else exists(step))
        def _():
            pl.semaphore_signal(barrier, inc=1, **at_recv(step))

    loads = [
        pltpu.make_async_copy(ids_in, ids, load_sem.at[0]),
        pltpu.make_async_copy(tapers_in, tapers, load_sem.at[1]),
        pltpu.make_async_copy(aperture_in, aperture, load_sem.at[2]),
        pltpu.make_async_copy(jitter_in, jitter, load_sem.at[3]),
        pltpu.make_async_copy(table_in, table, load_sem.at[4]),
    ]
    part = SRC // LOADS
    for p in range(LOADS):
        rows = pl.ds(p * part, part)
        loads.append(pltpu.make_async_copy(traces_in.at[rows], traces.at[rows], load_sem.at[5 + p]))
    for load in loads:
        load.start()

    for load in loads[:5]:
        load.wait()

    taper = jnp.zeros((SRC, TILE), I32)
    for a in range(SRC):
        taper = jnp.where(iota((SRC, TILE), 0) == a, tapers[a], taper)
    ramp = (iota((SRC, TILE), 1) - taper * 16).astype(F32) * (1.0 / 16.0)
    ramp = sine(jnp.clip(ramp, 0.0, 1.0) * (0.5 * math.pi))
    chosen = ramp * ramp

    lane = iota((8, TILE), 1)
    owner = jnp.zeros((8, TILE), I32)
    for a in range(SRC):
        owner = jnp.where((lane & 15) == a, ids[a] >> 4, owner)
    rank = jnp.zeros((8, TILE), I32)
    for a in range(SRC):
        rank = rank + ((owner == (ids[a] >> 4)) & ((lane & 15) > a)).astype(I32)
    shape = (SRC * 16, TILE)
    row, lane = iota(shape, 0), iota(shape, 1)
    same = (owner[:1] == (row >> 4)) & (rank[:1] == (row & 1)) & (((row >> 1) & 7) == (lane >> 4))
    pick[...] = same.astype(F32).astype(BF16)

    for a in range(0, SRC, 2):
        if a % part == 0:
            loads[5 + a // part].wait()
        both = [(traces[b].astype(F32) * chosen[b : b + 1, :]).astype(BF16) for b in (a, a + 1)]
        spectra = lax.dot_general(
            table[...], jnp.concatenate(both, axis=0), (((1,), (1,)), ((), ())), preferred_element_type=F32
        )
        for b in range(2):
            spec[pl.ds(a + b, 2 * FREQS, stride=SRC), :] = spectra[:, TILE * b : TILE * (b + 1)]

    wants = []
    for step in DIRS:
        reader = lax.rem(tile + step + tiles, tiles)
        want = jnp.int32(0)
        for g in range(APER):
            entry = aperture[g, reader]
            want = jnp.where((entry >= 0) & ((entry >> 2) == tile), entry & 3, want)
        wants.append(want)

    def split_strips(m, q, panel):
        quad = m * PER + q
        strips[quad] = panel.T.astype(BF16).reshape(STRIPS, STRIP, TILE)
        pieces = [strips[quad, s] for s in range(STRIPS)]
        for k in range(len(DIRS)):
            zsend[m, k, q] = choose(wants[k], range(STRIPS), pieces)

    def spec_panel(m, q):
        return spec[pl.ds(pl.multiple_of((m * PER + q) * TILE, TILE), TILE), :]

    def send_strips(first, count, group, which):
        chunks = pl.ds(first, count)
        for k in which:
            step = DIRS[k]

            @pl.when(exists(step))
            def _():
                pltpu.make_async_remote_copy(
                    zsend.at[chunks, k],
                    zrecv.at[chunks, len(DIRS) - 1 - k],
                    zsend_sem.at[k],
                    zrecv_sem.at[group, len(DIRS) - 1 - k],
                    **at_recv(step),
                ).start()

    def wait_strips(first, count, group):
        chunks = pl.ds(first, count)
        for k, step in enumerate(DIRS):

            @pl.when(exists(step))
            def _():
                pltpu.make_async_copy(zrecv.at[chunks, k], zrecv.at[chunks, k], zrecv_sem.at[group, k]).wait()

    def lay_rows(panels):
        slots = jnp.dot(pick[...], jnp.concatenate(panels, axis=1), preferred_element_type=F32).astype(BF16)
        return [slots[:, TILE * q : TILE * (q + 1)].reshape(SRC, 16, TILE) for q in range(PER)]

    def send_rows(first, count, group):
        chunks = pl.ds(first, count)
        for offset in OFFSETS:
            peer = shot_peer(offset)
            pltpu.make_async_remote_copy(
                asend.at[chunks, peer], arecv.at[chunks, me], asend_sem, arecv_sem.at[group], **at_shot(peer)
            ).start()

    def placed_rows(blocks):
        rows = jnp.dot(place[...], jnp.concatenate(blocks, axis=1), preferred_element_type=F32)
        return [rows[:, TILE * q : TILE * (q + 1)] for q in range(PER)]

    def lay_late(late):
        blocks = lay_rows([spec_panel(EARLY + late, q).astype(BF16) for q in range(PER)])
        for q in range(PER):
            first = 16 * (late * PER + q)
            bsend[:, first : first + 16, :] = blocks[q]

    for q in range(PER):
        split_strips(0, q, spec_panel(0, q))
    for late in range(LATE) if EAGER else ():
        lay_late(late)
    pl.semaphore_wait(barrier, peers)

    @pl.when(exists(-3) & slow(tile))
    def _():
        pl.semaphore_signal(ready, inc=1, **at_recv(-3))

    def send_near(group):
        first, count = GROUPS[group]
        send_strips(first, count, group, NEAR)

        @pl.when(jnp.logical_not(slow(tile + 3)))
        def _():
            send_strips(first, count, group, FAR)

    send_near(0)
    for late in range(LATE) if not EAGER else ():
        lay_late(late)
    for offset in OFFSETS:
        peer = shot_peer(offset)
        for late in range(LATE):
            rows = pl.ds(late * PER * 16, PER * 16)
            pltpu.make_async_remote_copy(
                bsend.at[peer, rows], brecv.at[me, rows], bsend_sem, brecv_sem, **at_shot(peer)
            ).start()
    brecv[me] = bsend[me]
    for group in range(1, len(GROUPS)):
        first, count = GROUPS[group]
        for m in range(first, first + count):
            for q in range(PER):
                split_strips(m, q, spec_panel(m, q))
        send_near(group)

    row, lane = iota((SRC, TILE), 0), iota((SRC, TILE), 1)
    label = jnp.full((SRC, TILE), -1, I32)
    count = jnp.zeros((SRC, TILE), I32)
    for a in range(SRC):
        hit = row == (ids[a] >> 4)
        label = jnp.where(hit & (count == (lane & 1)), ids[a] & 15, label)
        count = count + hit.astype(I32)
    for t in range(SRC):
        lsend[t] = label[t : t + 1, :]
    lrecv[me] = lsend[me]
    for offset in OFFSETS:
        peer = shot_peer(offset)
        pltpu.make_async_remote_copy(
            lsend.at[peer], lrecv.at[me], label_sem.at[0], label_sem.at[1], **at_shot(peer)
        ).start()

    row, lane = iota((STRIP, TILE), 0), iota((STRIP, TILE), 1)
    here = pl.ds(pl.multiple_of(tile * TILE, TILE), TILE)
    local_x = (tile * TILE + lane).astype(F32) + 0.4 * jitter[0:1, here]
    local_y = 3.0 * jitter[1:2, here]
    near = (0,) + DIRS
    jitters = []
    for step in near:
        there = lax.rem(tile + step + tiles, tiles)
        jitters.append(jitter[:, pl.ds(pl.multiple_of(there * TILE, TILE), TILE)])
    sources = []
    for g in range(APER):
        entry = aperture[g, tile]
        live = (entry >= 0).astype(F32)
        sources.append(jnp.where(entry >= 0, (entry >> 2) - tile, 0))
        strip = jnp.maximum(entry, 0)
        there = choose(sources[g], near, jitters)
        mask = lane == row + (strip & 3) * STRIP
        strip_x = jnp.sum(jnp.where(mask, there[0:1], 0.0), axis=1, keepdims=True)
        strip_y = jnp.sum(jnp.where(mask, there[1:2], 0.0), axis=1, keepdims=True)
        dx = (strip * STRIP + row).astype(F32) + 0.4 * strip_x - local_x
        dy = 3.0 * strip_y - local_y
        square = dx * dx + dy * dy
        cut = jnp.minimum(jnp.sqrt(square) * (1.0 / ((HALF + 1) * TILE)), 1.0)
        amp = cosine(cut * (0.5 * math.pi)) * (live / math.sqrt(APER * STRIP))
        turns = jnp.sqrt(square + 64.0) * (0.5 / 32.0)
        quarter = (turns - jnp.floor(turns + 0.5)) * math.pi
        sin_q, cos_q = sine(quarter), cosine(quarter)
        half = (1.0 - 2.0 * sin_q * sin_q, 2.0 * sin_q * cos_q)
        whole = plus(half, half)
        now = half
        for j in range(4):
            base[g, j, 0] = amp * now[0]
            base[g, j, 1] = amp * now[1]
            if j < 3:
                now = plus(now, whole)
        two = plus(whole, whole)
        four = plus(two, two)
        eight = plus(four, four)
        state[g, 0], state[g, 1] = four
        turn[g, 0], turn[g, 1] = eight

    @pl.when(exists(3) & slow(tile + 3))
    def _():
        pl.semaphore_wait(ready, 1)
        for group, (first, count) in enumerate(GROUPS):
            send_strips(first, count, group, FAR)

    own_strip = aperture[0, tile] & 3

    def make_green(m, carry):
        for g in range(APER):
            rows = pl.ds(g * STRIP, STRIP)
            cos_a, sin_a = state[g, 0], state[g, 1]
            for j in range(4):
                cos_b, sin_b = base[g, j, 0], base[g, j, 1]
                cc, ss, sc, cs = cos_a * cos_b, sin_a * sin_b, sin_a * cos_b, cos_a * sin_b
                green[m, 4 + j, rows, 0:TILE] = (cc - ss).astype(BF16)
                green[m, 4 + j, rows, TILE : 2 * TILE] = (-sc - cs).astype(BF16)
                green[m, 3 - j, rows, 0:TILE] = (cc + ss).astype(BF16)
                green[m, 3 - j, rows, TILE : 2 * TILE] = (cs - sc).astype(BF16)
            state[g, 0], state[g, 1] = plus((cos_a, sin_a), (turn[g, 0], turn[g, 1]))
        return carry

    lax.fori_loop(0, EARLY, make_green, 0)

    def product(m):
        panels = []
        for q in range(PER):
            own = choose(own_strip, range(STRIPS), [strips[m * PER + q, s] for s in range(STRIPS)])
            pieces = [own]
            options = [own] + [zrecv[m, k, q] for k in range(len(DIRS))]
            for g in range(1, APER):
                pieces.append(choose(sources[g], near, options))
            panel = jnp.concatenate(pieces, axis=0).T
            parts = []
            for f in range(4):
                both = jnp.dot(
                    panel[2 * SRC * f : 2 * SRC * (f + 1)], green[m, 4 * q + f], preferred_element_type=F32
                )
                parts.append(both[:SRC, :TILE] - both[SRC:, TILE:])
                parts.append(both[:SRC, TILE:] + both[SRC:, :TILE])
            panels.append(jnp.concatenate(parts, axis=0).astype(BF16))
        return panels

    def store(m, panels):
        for q in range(PER):
            panel = panels[q].astype(BF16).reshape(4, 2, SRC, TILE)
            for c in range(2):
                out[c, pl.ds((m * PER + q) * 4, 4)] = panel[:, c]

    def early(m, carry):
        blocks = lay_rows(product(m))
        for q in range(PER):
            asend[m, :, 16 * q : 16 * (q + 1), :] = blocks[q]
        arecv[m, me] = asend[m, me]
        return carry

    def early_group(group):
        first, count = GROUPS[group]
        wait_strips(first, count, group)
        lax.fori_loop(first, first + count, early, 0)
        send_rows(first, count, group)

    for group in range(SHIFT):
        early_group(group)

    most = lrecv.at[pl.ds(0, SRC - 1)]
    pltpu.make_async_copy(most, most, label_sem.at[1]).wait()
    row, lane = iota((TILE, TILE), 0), iota((TILE, TILE), 1)
    for h in range(2):
        label = jnp.zeros((1, TILE), I32)
        for j in range(8):
            label = jnp.where(iota((1, TILE), 1) >> 4 == j, lrecv[8 * h + j], label)
        same = (label == (row & 15)) & (((lane >> 1) & 7) == (row >> 4))
        place[:, TILE * h : TILE * (h + 1)] = same.astype(F32).astype(BF16)

    most = brecv.at[pl.ds(0, SRC - 1)]
    pltpu.make_async_copy(most, most, brecv_sem).wait()

    def relay(m, carry):
        first = pl.multiple_of((m - EARLY) * PER * 16, PER * 16)
        rows = brecv[:, pl.ds(first, PER * 16), :]
        rows = placed_rows([rows[:, 16 * q : 16 * (q + 1)].reshape(SRC * 16, TILE) for q in range(PER)])
        for q in range(PER):
            split_strips(m, q, rows[q])
        send_strips(m, 1, m - EARLY + len(GROUPS), ALL)
        return carry

    lax.fori_loop(EARLY, CHUNKS, relay, 0)
    for group in range(SHIFT, len(GROUPS)):
        early_group(group)

    lax.fori_loop(EARLY, CHUNKS, make_green, 0)

    def finish(m, carry):
        store(m, placed_rows([arecv[m, :, 16 * q : 16 * (q + 1), :].reshape(SRC * 16, TILE) for q in range(PER)]))
        return carry

    def finish_group(group):
        first, count = GROUPS[group]
        most = arecv.at[pl.ds(first, count), pl.ds(0, SRC - 1)]
        pltpu.make_async_copy(most, most, arecv_sem.at[group]).wait()
        lax.fori_loop(first, first + count, finish, 0)

    for group in range(HOLD):
        finish_group(group)

    def late(m, carry):
        wait_strips(m, 1, m - EARLY + len(GROUPS))
        store(m, product(m))
        return carry

    lax.fori_loop(EARLY, CHUNKS, late, 0)
    for group in range(HOLD, len(GROUPS)):
        finish_group(group)

    for k, step in enumerate(DIRS):

        @pl.when(exists(step))
        def _():
            pltpu.make_async_copy(zsend.at[:, k], zsend.at[:, k], zsend_sem.at[k]).wait()

    most = lsend.at[pl.ds(0, SRC - 1)]
    pltpu.make_async_copy(most, most, label_sem.at[0]).wait()
    most = asend.at[:, pl.ds(0, SRC - 1)]
    pltpu.make_async_copy(most, most, asend_sem).wait()
    most = bsend.at[pl.ds(0, SRC - 1)]
    pltpu.make_async_copy(most, most, bsend_sem).wait()


def dft_table():
    samples = np.arange(TILE)[None, :]
    bins = np.arange(FREQS)[:, None]
    angle = np.pi * ((2 * bins + 1) * samples % (2 * TILE)) / TILE
    values = np.stack([np.cos(angle), -np.sin(angle)], axis=1) / math.sqrt(TILE)
    return values.reshape(2 * FREQS, TILE)


def local(tiles, traces, source_ids, taper_ids, recv_jitter, aperture):
    hbm = pl.BlockSpec(memory_space=pltpu.HBM)
    table = jnp.asarray(dft_table(), BF16)
    dirs = len(DIRS)
    return pl.pallas_call(
        functools.partial(kernel, tiles),
        out_shape=pltpu.VMEM((2, FREQS, SRC, TILE), BF16),
        in_specs=[hbm] * 6,
        out_specs=pl.BlockSpec(memory_space=pltpu.VMEM),
        scratch_shapes=[
            pltpu.SMEM((SRC,), I32),
            pltpu.SMEM((SRC,), I32),
            pltpu.SMEM((APER, tiles), I32),
            pltpu.VMEM(recv_jitter.shape, F32),
            pltpu.VMEM(traces.shape, BF16),
            pltpu.VMEM(table.shape, BF16),
            pltpu.VMEM((2 * FREQS * SRC, TILE), F32),
            pltpu.VMEM((QUADS, STRIPS, STRIP, TILE), BF16),
            pltpu.VMEM((CHUNKS, dirs, PER, STRIP, TILE), BF16),
            pltpu.VMEM((CHUNKS, dirs, PER, STRIP, TILE), BF16),
            pltpu.VMEM((APER, 4, 2, STRIP, TILE), F32),
            pltpu.VMEM((APER, 2, STRIP, TILE), F32),
            pltpu.VMEM((APER, 2, STRIP, TILE), F32),
            pltpu.VMEM((CHUNKS, 8, APER * STRIP, 2 * TILE), BF16),
            pltpu.VMEM((SRC * 16, TILE), BF16),
            pltpu.VMEM((TILE, SRC * 16), BF16),
            pltpu.VMEM((SRC, 1, TILE), I32),
            pltpu.VMEM((SRC, 1, TILE), I32),
            pltpu.VMEM((EARLY, SRC, 16 * PER, TILE), BF16),
            pltpu.VMEM((EARLY, SRC, 16 * PER, TILE), BF16),
            pltpu.VMEM((SRC, LATE * 16 * PER, TILE), BF16),
            pltpu.VMEM((SRC, LATE * 16 * PER, TILE), BF16),
            pltpu.SemaphoreType.DMA((5 + LOADS,)),
            pltpu.SemaphoreType.DMA((dirs,)),
            pltpu.SemaphoreType.DMA((len(GROUPS) + LATE, dirs)),
            pltpu.SemaphoreType.DMA((2,)),
            pltpu.SemaphoreType.DMA,
            pltpu.SemaphoreType.DMA((len(GROUPS),)),
            pltpu.SemaphoreType.DMA,
            pltpu.SemaphoreType.DMA,
            pltpu.SemaphoreType.REGULAR,
        ],
        compiler_params=pltpu.CompilerParams(
            collective_id=0, has_side_effects=True, vmem_limit_bytes=62 * 1024 * 1024
        ),
    )(source_ids, taper_ids, aperture.T, recv_jitter, traces, table)


def solution(mesh):
    placed = (P("shot", "recv", None), P("shot"), P("shot"), P(), P())
    return jax.shard_map(
        functools.partial(local, mesh.shape["recv"]),
        mesh=mesh,
        in_specs=placed,
        out_specs=P(None, None, "shot", "recv"),
        check_vma=False,
    )
```
